512 devices in a mesh: blk: 16 (over x, z_lo), wide: 32 (over y, z_hi, core).
Axes of the slice: x: 4, y: 8, z: 8 (z_hi: 2, z_lo: 4; z = z_hi * 4 + z_lo), core: 2. Of those that a mesh axis runs over, the one named last changes fastest.
Arguments:
- y_first: bfloat16 [32, 2048, 1536], P('wide', 'blk'), may hold values from -6 to 6
- y_second: bfloat16 [32, 2048, 1536], P('wide', 'blk'), may hold values from -6 to 6
- first_output_cotangent: bfloat16 [32, 2048, 1536], P('wide', 'blk'), may hold values from -6 to 6
- dy_second: bfloat16 [32, 2048, 1536], P('wide', 'blk'), may hold values from -4 to 4
- in_proj: bfloat16 [3, 1536, 768], P(None, 'wide'), may hold values from -1 to 1
- out_proj: bfloat16 [768, 1536], P(None, 'wide'), may hold values from -0.21875 to 0.21875
Outputs:
- x_first: bfloat16 [32, 2048, 1536], P('wide', 'blk')
- dx_second: bfloat16 [32, 2048, 1536], P('wide', 'blk')
- grad_out_proj: float32 [768, 1536], P('blk', 'wide')
The draws below stay inside these ranges and needn't reach their ends.
All inputs are finite; a program needn't handle non-finite values.
Results may differ from the reference program's by a relative error of at most 0.03.
Values may be sent and summed in bfloat16 or wider, within the bound.
A program may use at most 64 MiB of HBM per device.

```python
from functools import partial
import jax
import jax.numpy as jnp
from jax import lax

D = 1536
HDIM = 64
HW = 768
BLOCK_TOKENS = 128
SEQ = 2048
SLIDES = 32


def draw_in_proj(key, part):
    key = jax.random.fold_in(key, 7)
    base_key, value_key = jax.random.split(key, 2)
    spread = D ** (-0.5)
    paired = jnp.clip(jax.random.normal(base_key, (2, D, HW), jnp.float32), -4.0, 4.0) * 1.5 * spread
    queries = paired[0]
    keyset = paired[1]
    valset = jnp.clip(jax.random.normal(value_key, (D, HW), jnp.float32), -4.0, 4.0) * spread
    stacked = jnp.clip(jnp.stack([queries, keyset, valset]), -1.0, 1.0)
    return stacked.astype(jnp.bfloat16)


def strengthened(entries, own_key, source, target, blocks, factor):
    def block_of(position):
        return (jnp.arange(entries.shape[position]) // (entries.shape[position] // blocks)).reshape((-1,) + (1,) * (entries.ndim - 1 - position))

    first = jax.random.permutation(own_key, blocks)[block_of(target)]
    second = (block_of(target) + blocks // 2) % blocks
    return jnp.where((block_of(source) == first) | (block_of(source) == second), factor * entries, entries)


def block_levels(own_key, extent, cuts, smallest, high):
    loudness, own = 1.0, jax.random.fold_in(own_key, 6)
    for dim, blocks in cuts:
        draws = jnp.exp(jax.random.uniform(jax.random.fold_in(own, dim), (blocks,), jnp.float32, smallest / len(cuts), high / len(cuts)))
        loudness = loudness * jnp.repeat(draws, extent[dim] // blocks).reshape([-1 if axis == dim else 1 for axis in range(len(extent))])
    return loudness


def centred(stream_key, shape, scale, bound, cuts=(), kind=jnp.bfloat16):
    values = scale * jax.random.normal(stream_key, shape, jnp.float32)
    if cuts:
        values = values * block_levels(stream_key, shape, cuts, -0.22, 0.18)
    return jnp.clip(values, -bound, bound).astype(kind)


def noise_with(own_key, dims, scale, limit, cuts, heavy, kind=jnp.bfloat16):
    drawn = scale * jax.random.normal(own_key, dims, jnp.float32)
    if cuts:
        drawn = drawn * block_levels(own_key, dims, cuts, -0.22, 0.18)
    return jnp.clip(strengthened(drawn, jax.random.fold_in(own_key, 3), *heavy), -limit, limit).astype(kind)


def setup_inputs(seed: int = 0) -> dict:
    streams_of = jax.random.split(jax.random.key(seed), 7)
    y_first = centred(streams_of[0], (SLIDES, SEQ, D), 0.5, 6.0, ((0, 32), (1, 16)))
    y_second = centred(streams_of[1], (SLIDES, SEQ, D), 1.0, 6.0, ((0, 32), (1, 16)))
    first_output_cotangent = noise_with(streams_of[2], (SLIDES, SEQ, D), 1.0, 6.0, ((0, 32), (1, 16)), (0, 2, 32, 2.75))
    dy_second = centred(streams_of[3], (SLIDES, SEQ, D), 0.3, 4.0, ((0, 32), (1, 16)))
    in_proj = draw_in_proj(jax.random.fold_in(streams_of[6], 71), 0)
    out_proj = centred(streams_of[5], (HW, D), HW ** -0.5, 0.21875, ((1, 32),))
    return dict(y_first=y_first, y_second=y_second, first_output_cotangent=first_output_cotangent, dy_second=dy_second, in_proj=in_proj, out_proj=out_proj)


OFFSETS = (-2, -1, 0, 1, 2)
EPSILON = 1e-05

def rounded_length(values):
    return lax.optimization_barrier(values.astype(jnp.bfloat16))

def normalize(values):
    values = values.astype(jnp.float32)
    center = values - lax.optimization_barrier(jnp.mean(values, axis=-1, keepdims=True))
    inv_std = lax.rsqrt(lax.optimization_barrier(jnp.mean(center * center, axis=-1, keepdims=True)) + EPSILON)
    return (center * inv_std, inv_std)

def gather_window(blocks):
    stacked = jnp.stack([jnp.roll(blocks, -offset, axis=0) for offset in OFFSETS], axis=1)
    return stacked.reshape((blocks.shape[0], -1) + blocks.shape[2:])

def window_back(parts):
    split = parts.reshape((parts.shape[0], len(OFFSETS), -1) + parts.shape[2:]).astype(jnp.float32)
    summed = jnp.zeros(split[:, 0].shape, jnp.float32)
    for index, offset in enumerate(OFFSETS):
        summed = summed + jnp.roll(split[:, index], offset, axis=0)
    return rounded_length(summed)

def one_slide(streams, in_proj, out_proj):
    y_first, y_second, first_output_cotangent, dy_second = streams
    seq_len = y_second.shape[0]
    number_of_blocks = seq_len // BLOCK_TOKENS
    hidden_features = in_proj.shape[2]
    head_count = hidden_features // HDIM
    scale = HDIM ** (-0.5)
    unit, inv_std = normalize(y_second)
    unit_b = rounded_length(unit)
    projected = rounded_length(jnp.einsum('sd,cdh->csh', unit_b.astype(jnp.float32), in_proj.astype(jnp.float32)))
    shape = (number_of_blocks, BLOCK_TOKENS, head_count, HDIM)
    queries = projected[0].reshape(shape).astype(jnp.float32)
    keyset = gather_window(projected[1].reshape(shape)).astype(jnp.float32)
    valset = gather_window(projected[2].reshape(shape)).astype(jnp.float32)
    scores = jnp.einsum('bqhd,bkhd->bhqk', queries, keyset) * scale
    attn_weights = jax.nn.softmax(scores, axis=-1)
    weights_b = rounded_length(attn_weights).astype(jnp.float32)
    mixture = rounded_length(jnp.einsum('bhqk,bkhd->bqhd', weights_b, valset))
    flattened_mixture = mixture.reshape(seq_len, hidden_features)
    branch = jnp.dot(flattened_mixture, out_proj, preferred_element_type=jnp.float32)
    x_first = (y_first.astype(jnp.float32) - branch).astype(jnp.bfloat16)
    d_mixture = rounded_length(jnp.dot(first_output_cotangent, out_proj.T, preferred_element_type=jnp.float32))
    per_block_gradients = rounded_length(jnp.einsum('zen,zew->znw', flattened_mixture.reshape(number_of_blocks, BLOCK_TOKENS, hidden_features).astype(jnp.float32), first_output_cotangent.reshape(number_of_blocks, BLOCK_TOKENS, -1).astype(jnp.float32)))
    slide_grad = lax.optimization_barrier(jnp.sum(per_block_gradients.astype(jnp.float32), axis=0)).astype(jnp.bfloat16)
    dm_heads = d_mixture.reshape(shape).astype(jnp.float32)
    delta = lax.optimization_barrier(jnp.sum(dm_heads * mixture.astype(jnp.float32), axis=-1))
    d_weights = jnp.einsum('bqhd,bkhd->bhqk', dm_heads, valset)
    d_scores = rounded_length(attn_weights * (d_weights - jnp.transpose(delta, (0, 2, 1))[..., None]) * scale).astype(jnp.float32)
    d_queries = rounded_length(jnp.einsum('bhqk,bkhd->bqhd', d_scores, keyset))
    key_parts = rounded_length(jnp.einsum('bhqk,bqhd->bkhd', d_scores, queries))
    value_parts = rounded_length(jnp.einsum('bhqk,bqhd->bkhd', weights_b, dm_heads))
    d_keys = window_back(key_parts)
    d_values = window_back(value_parts)
    grads_all = jnp.stack([d_queries.reshape(seq_len, hidden_features), d_keys.reshape(seq_len, hidden_features), d_values.reshape(seq_len, hidden_features)])
    d_unit = jnp.einsum('csh,cdh->sd', grads_all.astype(jnp.float32), in_proj.astype(jnp.float32))
    correction = d_unit - lax.optimization_barrier(jnp.mean(d_unit, axis=-1, keepdims=True)) - unit * lax.optimization_barrier(jnp.mean(d_unit * unit, axis=-1, keepdims=True))
    dx_second = (dy_second.astype(jnp.float32) + inv_std * correction).astype(jnp.bfloat16)
    return (x_first, dx_second, slide_grad)

def reference(y_first, y_second, first_output_cotangent, dy_second, in_proj, out_proj):
    x_first, dx_second, slide_grads = lax.map(partial(one_slide, in_proj=in_proj, out_proj=out_proj), (y_first, y_second, first_output_cotangent, dy_second))
    grad_out_proj = lax.optimization_barrier(jnp.sum(slide_grads.astype(jnp.float32), axis=0)) / SLIDES
    return (x_first, dx_second, grad_out_proj)
```

```python
import functools

import jax
import jax.numpy as jnp
from jax import lax
from jax.experimental import pallas as pl
from jax.experimental.pallas import tpu as pltpu
from jax.sharding import PartitionSpec as P

HDIM = 64
MESH = pl.DeviceIdType.MESH
F32 = jnp.float32
BF16 = jnp.bfloat16


OFFSETS = (-2, -1, 0, 1, 2)
EPSILON = 1e-05


def passed_along(block, axis, distance):
    devices = range(lax.axis_size(axis))
    route = [((i - distance) % len(devices), i) for i in devices]
    return lax.ppermute(block, axis, route)


def normalize(values):
    values = values.astype(jnp.float32)
    center = values - jnp.mean(values, axis=-1, keepdims=True)
    inv_std = lax.rsqrt(jnp.mean(center * center, axis=-1, keepdims=True) + EPSILON)
    return (center * inv_std, inv_std)


def fetch_window(stacked):
    pieces = {0: stacked}
    for offset in (2, 1, -1, -2):
        pieces[-offset] = passed_along(stacked, "blk", offset)
    return jnp.concatenate([pieces[offset] for offset in OFFSETS], axis=1)


def return_grads(parts):
    summed = parts[:, 2].astype(jnp.float32)
    for offset in (2, 1, -1, -2):
        arrived = passed_along(parts[:, offset + 2], "blk", offset)
        summed = summed + arrived.astype(jnp.float32)
    return summed.astype(jnp.bfloat16)


def attend(queries, window, head_count):
    tokens = queries.shape[0]
    keyset = window[0].reshape(-1, head_count, HDIM)
    valset = window[1].reshape(-1, head_count, HDIM)
    scores = jnp.einsum(
        "qhd,khd->hqk",
        queries.reshape(tokens, head_count, HDIM),
        keyset,
        preferred_element_type=jnp.float32,
    ) * HDIM ** (-0.5)
    attn_weights = jax.nn.softmax(scores, axis=-1)
    weights_b = attn_weights.astype(jnp.bfloat16)
    mixture = jnp.einsum(
        "hqk,khd->qhd", weights_b, valset, preferred_element_type=jnp.float32
    ).astype(jnp.bfloat16)
    return (attn_weights, weights_b, mixture.reshape(tokens, head_count * HDIM))


STEPS = ((4, 3), (3, 4))


def gather_kernel(second_ref, upstream_ref, in_ref, out_ref, w_ref, proj_ref,
                  lhs, acc, far_send, near_send, far_recv, ring_send, ring_recv,
                  core_send, core_recv):
    b, w = lax.axis_index("blk"), lax.axis_index("wide")
    zl, y, zh, c = b % 4, w // 4, (w // 2) % 2, w % 2
    edge = (zl == 0) | (zl == 3)
    above = {"wide": ((y + 1) % 8) * 4 + zh * 2 + c}
    below = {"wide": ((y + 7) % 8) * 4 + zh * 2 + c}
    partner = {"wide": w + 1 - 2 * c}
    far = {"blk": b + 3 - 2 * zl, "wide": w + 2 - 4 * zh}
    near = {"blk": b + 1 - 2 * (b % 2)}
    half = (zh, 1 - zh)

    barrier = pltpu.get_barrier_semaphore()
    for device in (above, below, partner, near):
        pl.semaphore_signal(barrier, inc=1, device_id=device, device_id_type=MESH)

    @pl.when(edge)
    def _():
        pl.semaphore_signal(barrier, inc=1, device_id=far, device_id_type=MESH)

    for m in range(3):
        w_ref[m, y, zh, c] = in_ref[m]
    w_ref[3, y, zh, c] = out_ref[...]
    pl.semaphore_wait(barrier, 4 + edge.astype(jnp.int32))

    def copy(block, send, recv, device):
        return pltpu.make_async_remote_copy(
            src_ref=block, dst_ref=block, send_sem=send, recv_sem=recv,
            device_id=device, device_id_type=MESH)

    def far_copy(m, q):
        return copy(w_ref.at[m, y, half[q], c], far_send.at[m], far_recv.at[m], far)

    def near_copy(m):
        return copy(w_ref.at[m, y, half[1], c], near_send.at[m], far_recv.at[m], near)

    def ring_copy(m, q, way, s):
        origin = (y + 8 - s) % 8 if way == 0 else (y + s) % 8
        return copy(w_ref.at[m, origin, half[q], c], ring_send.at[m, q, way, s],
                    ring_recv.at[m, q, way, s], above if way == 0 else below)

    def arrived(m, q, way, s):
        origin = (y + 7 - s) % 8 if way == 0 else (y + 1 + s) % 8
        return copy(w_ref.at[m, origin, half[q], c], ring_send.at[m, q, way, s],
                    ring_recv.at[m, q, way, s], above if way == 0 else below)

    def core_copy(m, q, j, origin, core):
        return copy(w_ref.at[m, origin, half[q], core], core_send.at[m, q, j],
                    core_recv.at[m, q, j], partner)

    def place(way, s):
        return (y + 7 - s) % 8 if way == 0 else (y + 1 + s) % 8

    def slot(way, s):
        return 4 if s == 3 else (1 + s if way == 0 else 5 + s)

    def send_own(m):
        for way in range(2):
            ring_copy(m, 0, way, 0).start()
        core_copy(m, 0, 0, y, c).start()

    def pass_near(m):
        far_copy(m, 1).wait_recv()
        near_copy(m).start()

    @pl.when(edge)
    def _():
        for m in range(4):
            far_copy(m, 0).start()

    send_own(0)

    values = second_ref[0].astype(F32)
    center = values - jnp.mean(values, axis=-1, keepdims=True)
    inv_std = lax.rsqrt(jnp.mean(center * center, axis=-1, keepdims=True) + EPSILON)
    unit_b = (center * inv_std).astype(BF16)
    upstream = upstream_ref[0]
    for i in range(8):
        lhs[0, i] = unit_b[:, 192 * i:192 * i + 192]
        lhs[1, i] = upstream[:, 192 * i:192 * i + 192]

    @pl.when(edge)
    def _():
        pass_near(0)

    def one(m, _):
        side = m // 3

        def compute(j, origin, first=False):
            for q in range(2):
                core_copy(m, q, j, origin, 1 - c).wait_recv()
            term = jnp.dot(lhs[side, origin], w_ref[m, origin].reshape(192, 768),
                           preferred_element_type=F32)
            if first:
                acc[...] = term
            else:
                acc[...] += term

        @pl.when(jnp.logical_not(edge))
        def _():
            far_copy(m, 1).wait_recv()

        for way in range(2):
            ring_copy(m, 1, way, 0).start()
        core_copy(m, 1, 0, y, c).start()
        for s in range(4):
            for q in range(2):
                for way in range(2):
                    if s < STEPS[q][way]:
                        arrived(m, q, way, s).wait_recv()
                        if s + 1 < STEPS[q][way]:
                            ring_copy(m, q, way, s + 1).start()
                        core_copy(m, q, slot(way, s), place(way, s), c).start()
            if s == 1:
                @pl.when(m < 3)
                def _():
                    send_own(m + 1)

                @pl.when((m < 3) & edge)
                def _():
                    pass_near(m + 1)
            if s == 0:
                compute(0, y, True)
            else:
                for way in range(2):
                    compute(slot(way, s - 1), place(way, s - 1))
        compute(4, place(0, 3))
        proj_ref[m] = acc[...].astype(BF16)
        return 0

    lax.fori_loop(0, 4, one, 0)

    def drain(m, _):
        @pl.when(edge)
        def _():
            far_copy(m, 0).wait_send()
            near_copy(m).wait_send()

        for q in range(2):
            for way in range(2):
                for s in range(STEPS[q][way]):
                    ring_copy(m, q, way, s).wait_send()
            for j in range(8):
                core_copy(m, q, j, y, c).wait_send()
        return 0

    lax.fori_loop(0, 4, drain, 0)


def gather_project(y_second, upstream, in_proj, out_t):
    vmem = pl.BlockSpec(memory_space=pltpu.VMEM)
    dma = pltpu.SemaphoreType.DMA
    return pl.pallas_call(
        gather_kernel,
        out_shape=(jax.ShapeDtypeStruct((4, 8, 2, 2, 48, 768), BF16),
                   jax.ShapeDtypeStruct((4, 128, 768), BF16)),
        in_specs=[vmem] * 4,
        out_specs=(vmem, vmem),
        scratch_shapes=[
            pltpu.VMEM((2, 8, 128, 192), BF16),
            pltpu.VMEM((128, 768), F32),
            dma((4,)), dma((4,)), dma((4,)),
            dma((4, 2, 2, 4)), dma((4, 2, 2, 4)),
            dma((4, 2, 8)), dma((4, 2, 8)),
        ],
        compiler_params=pltpu.CompilerParams(
            collective_id=0, has_side_effects=True, vmem_limit_bytes=48 * 2**20),
        name="gather_project",
    )(y_second, upstream, in_proj, out_t)


def body(y_first, y_second, first_output_cotangent, dy_second, in_proj, out_proj):
    whole, proj = gather_project(y_second, first_output_cotangent, in_proj, out_proj.T)
    whole = whole.reshape(4, 1536, 768)
    whole_in, whole_out = whole[:3], whole[3]
    hidden_features = whole_in.shape[2]
    head_count = hidden_features // HDIM
    unit, inv_std = normalize(y_second[0])
    queries, stacked = proj[0], proj[1:3]
    tokens = queries.shape[0]
    window = fetch_window(stacked)
    attn_weights, weights_b, mixture = attend(queries, window, head_count)
    branch = jnp.einsum("sh,dh->sd", mixture, whole_out, preferred_element_type=jnp.float32)
    x_first = (y_first[0].astype(jnp.float32) - branch).astype(jnp.bfloat16)
    upstream = first_output_cotangent[0]
    d_mixture = proj[3]
    dm_heads = d_mixture.reshape(tokens, head_count, HDIM)
    delta = jnp.sum(
        dm_heads.astype(jnp.float32)
        * mixture.reshape(tokens, head_count, HDIM).astype(jnp.float32),
        axis=-1,
    )
    keyset = window[0].reshape(-1, head_count, HDIM)
    valset = window[1].reshape(-1, head_count, HDIM)
    d_weights = jnp.einsum("qhd,khd->hqk", dm_heads, valset, preferred_element_type=jnp.float32)
    d_scores = (attn_weights * (d_weights - delta.T[:, :, None]) * HDIM ** (-0.5)).astype(
        jnp.bfloat16
    )
    q_heads = queries.reshape(tokens, head_count, HDIM)
    d_queries = jnp.einsum(
        "hqk,khd->qhd", d_scores, keyset, preferred_element_type=jnp.float32
    ).astype(jnp.bfloat16)
    d_keys = jnp.einsum(
        "hqk,qhd->khd", d_scores, q_heads, preferred_element_type=jnp.float32
    ).astype(jnp.bfloat16)
    d_values = jnp.einsum(
        "hqk,qhd->khd", weights_b, dm_heads, preferred_element_type=jnp.float32
    ).astype(jnp.bfloat16)
    parts = jnp.stack([d_keys, d_values]).reshape(2, len(OFFSETS), tokens, hidden_features)
    returned = return_grads(parts)
    grads_all = jnp.concatenate([d_queries.reshape(1, tokens, hidden_features), returned], axis=0)
    d_unit = jnp.einsum("csh,cdh->sd", grads_all, whole_in, preferred_element_type=jnp.float32)
    correction = (
        d_unit
        - jnp.mean(d_unit, axis=-1, keepdims=True)
        - unit * jnp.mean(d_unit * unit, axis=-1, keepdims=True)
    )
    dx_second = (dy_second[0].astype(jnp.float32) + inv_std * correction).astype(jnp.bfloat16)
    dwo_term = jnp.einsum("sh,sd->hd", mixture, upstream, preferred_element_type=jnp.float32)
    block_summed = lax.psum_scatter(
        dwo_term.astype(jnp.bfloat16), "blk", scatter_dimension=0, tiled=True
    )
    slide_summed = lax.psum_scatter(block_summed, "wide", scatter_dimension=1, tiled=True).astype(
        jnp.float32
    )
    grad_out_proj = slide_summed / lax.axis_size("wide")
    return (x_first[None], dx_second[None], grad_out_proj)


def solution(mesh):
    placed = (
        P("wide", "blk", None),
        P("wide", "blk", None),
        P("wide", "blk", None),
        P("wide", "blk", None),
        P(None, "wide", None),
        P(None, "wide"),
    )
    return jax.shard_map(
        body,
        mesh=mesh,
        in_specs=placed,
        out_specs=(P("wide", "blk", None), P("wide", "blk", None), P("blk", "wide")),
        check_vma=False,
    )
```

```python
import functools

import jax
import jax.numpy as jnp
from jax import lax
from jax.experimental import pallas as pl
from jax.experimental.pallas import tpu as pltpu
from jax.sharding import PartitionSpec as P

HDIM = 64
EPSILON = 1e-05
MESH = pl.DeviceIdType.MESH
F32 = jnp.float32
BF16 = jnp.bfloat16

STEPS = ((4, 3), (3, 4))
KEY, VALUE, QUERY, OUT = range(4)
MIX, DQ, DK, DV = range(4)


def nt(a, b):
    return lax.dot_general(a, b, (((1,), (1,)), ((), ())), preferred_element_type=F32)


def nn(a, b):
    return jnp.dot(a, b, preferred_element_type=F32)


def kernel(first_ref, second_ref, upstream_ref, dsecond_ref, in_ref, out_ref,
           x_ref, dx_ref, grad_ref,
           wall, lhs, acc, proj, recv, kn, vn, kt, vt, probs, mix, dq, dkv, halo_out,
           halo_in, dkv_out, back, d_unit, up_half, up_other, mix_other, xs, xr, ys, yr, zs, zr,
           far_send, near_send, far_recv, ring_send, ring_recv, core_send, core_recv,
           swap_send, swap_recv, spread_send, spread_recv, halo_send, halo_recv,
           ghalo_send, ghalo_recv, back_send, back_recv,
           xs_send, xs_recv, ys_send, ys_recv, zs_send, zs_recv):
    b, w = lax.axis_index("blk"), lax.axis_index("wide")
    x, zl, y, zh, c = b // 4, b % 4, w // 4, (w // 2) % 2, w % 2
    edge = (zl == 0) | (zl == 3)
    half = (zh, 1 - zh)

    def at_x(d):
        return {"blk": ((x + d) % 4) * 4 + zl}

    def at_y(d):
        return {"wide": ((y + d) % 8) * 4 + zh * 2 + c}

    def at_z(d, other):
        return {"blk": x * 4 + (zl + d) % 4, "wide": w + other * (2 - 4 * zh)}

    above, below = at_y(1), at_y(7)
    partner = {"wide": w + 1 - 2 * c}
    far = {"blk": b + 3 - 2 * zl, "wide": w + 2 - 4 * zh}
    near = {"blk": b + 1 - 2 * (b % 2)}

    def copy(src, dst, send, got, device):
        return pltpu.make_async_remote_copy(
            src_ref=src, dst_ref=dst, send_sem=send, recv_sem=got,
            device_id=device, device_id_type=MESH)

    barrier = pltpu.get_barrier_semaphore()
    greeted = [partner] + [at_x(d) for d in range(1, 4)] + [at_y(d) for d in range(1, 8)]
    greeted += [at_z(d, 0) for d in range(1, 4)] + [at_z(d, 1) for d in range(4)]
    for device in greeted:
        pl.semaphore_signal(barrier, inc=1, device_id=device, device_id_type=MESH)

    for m, source in ((KEY, 1), (VALUE, 2), (QUERY, 0)):
        wall[m, y, zh, c] = in_ref[source]
    wall[OUT, y, zh, c] = out_ref[...]
    pl.semaphore_wait(barrier, len(greeted))

    def far_copy(m, q):
        block = wall.at[m, y, half[q], c]
        return copy(block, block, far_send.at[m], far_recv.at[m], far)

    def near_copy(m):
        block = wall.at[m, y, half[1], c]
        return copy(block, block, near_send.at[m], far_recv.at[m], near)

    def ring_copy(m, q, way, s):
        origin = (y + 8 - s) % 8 if way == 0 else (y + s) % 8
        block = wall.at[m, origin, half[q], c]
        return copy(block, block, ring_send.at[m, q, way, s], ring_recv.at[m, q, way, s],
                    above if way == 0 else below)

    def place(way, s):
        return (y + 7 - s) % 8 if way == 0 else (y + 1 + s) % 8

    def arrived(m, q, way, s):
        block = wall.at[m, place(way, s), half[q], c]
        return copy(block, block, ring_send.at[m, q, way, s], ring_recv.at[m, q, way, s],
                    above if way == 0 else below)

    def core_copy(m, q, j, origin, core):
        block = wall.at[m, origin, half[q], core]
        return copy(block, block, core_send.at[m, q, j], core_recv.at[m, q, j], partner)

    def slot(way, s):
        return 4 if s == 3 else (1 + s if way == 0 else 5 + s)

    def send_own(m):
        for way in range(2):
            ring_copy(m, 0, way, 0).start()
        core_copy(m, 0, 0, y, c).start()

    def pass_near(m):
        far_copy(m, 1).wait_recv()
        near_copy(m).start()

    def spread_copy(m, d):
        return copy(proj.at[m, (zl + d) % 4], recv.at[m, 2 + zl], spread_send.at[m, d - 1],
                    spread_recv.at[m, d - 1], at_z(d, 0))

    def spread_arrived(m, d):
        return copy(proj.at[m, (zl + d) % 4], recv.at[m, 2 + (zl + 4 - d) % 4],
                    spread_send.at[m, d - 1], spread_recv.at[m, d - 1], at_z(d, 0))

    def halo_copy(m, way, arriving=False):
        start = (4, 2)[way]
        into = (0, 6)[way]
        return copy(recv.at[m, start:start + 2], recv.at[m, into:into + 2],
                    halo_send.at[m, way], halo_recv.at[m, way], at_x((1, 3)[way]))

    def ghalo_copy(kv, way):
        return copy(halo_out.at[kv, way], halo_in.at[kv, way], ghalo_send.at[kv, way],
                    ghalo_recv.at[kv, way], at_x((3, 1)[way]))

    def back_copy(t, source, j):
        return copy(source, back.at[t, zl], back_send.at[t, j], back_recv.at[t, zl],
                    {"blk": x * 4 + j})

    def send_back(t, source, j):
        @pl.when(j != zl)
        def _():
            back_copy(t, source, j).start()

        @pl.when(j == zl)
        def _():
            back[t, zl] = source[...]

    def wait_back(t):
        for d in range(1, 4):
            g = (zl + d) % 4
            copy(back.at[t, g], back.at[t, g], back_send.at[t, g], back_recv.at[t, g],
                 {"blk": x * 4 + g}).wait_recv()

    def other_half():
        return copy(up_half.at[1 - c], up_other, swap_send.at[0], swap_recv.at[0], partner)

    def other_mix():
        return copy(back.at[MIX], mix_other, swap_send.at[1], swap_recv.at[1], partner)

    def x_copy(d):
        return copy(xs.at[(x + d) % 4], xr.at[d - 1], xs_send.at[d - 1], xs_recv.at[d - 1], at_x(d))

    def y_copy(d):
        return copy(ys.at[(y + d) % 8], yr.at[d - 1], ys_send.at[d - 1], ys_recv.at[d - 1], at_y(d))

    def z_copy(d, other):
        n = d + 4 * other - 1
        return copy(zs.at[(zl + d) % 4], zr.at[n], zs_send.at[n], zs_recv.at[n], at_z(d, other))

    z_partners = [(d, 0) for d in range(1, 4)] + [(d, 1) for d in range(4)]

    @pl.when(edge)
    def _():
        for m in range(4):
            far_copy(m, 0).start()

    send_own(0)

    values = second_ref[0].astype(F32)
    center = values - jnp.mean(values, axis=-1, keepdims=True)
    inv_std = lax.rsqrt(jnp.mean(center * center, axis=-1, keepdims=True) + EPSILON)
    unit_b = (center * inv_std).astype(BF16)
    upstream = upstream_ref[0]
    for i in range(8):
        lhs[0, i] = unit_b[:, 192 * i:192 * i + 192]
        lhs[1, i] = upstream[:, 192 * i:192 * i + 192]
    by_core = upstream.T.reshape(16, 2, 48, 128)
    for core in range(2):
        up_half[core] = by_core[:, core].reshape(768, 128).T
    other_half().start()

    @pl.when(edge)
    def _():
        pass_near(0)

    def gather_one(m, _):
        side = m // 3

        def compute(j, origin, first=False):
            for q in range(2):
                core_copy(m, q, j, origin, 1 - c).wait_recv()
            term = nn(lhs[side, origin], wall[m, origin].reshape(192, 768))
            if first:
                acc[...] = term
            else:
                acc[...] += term

        @pl.when(jnp.logical_not(edge))
        def _():
            far_copy(m, 1).wait_recv()

        for way in range(2):
            ring_copy(m, 1, way, 0).start()
        core_copy(m, 1, 0, y, c).start()
        for s in range(4):
            for q in range(2):
                for way in range(2):
                    if s < STEPS[q][way]:
                        arrived(m, q, way, s).wait_recv()
                        if s + 1 < STEPS[q][way]:
                            ring_copy(m, q, way, s + 1).start()
                        core_copy(m, q, slot(way, s), place(way, s), c).start()
            if s == 1:
                @pl.when(m < 3)
                def _():
                    send_own(m + 1)

                @pl.when((m < 3) & edge)
                def _():
                    pass_near(m + 1)
            if s == 2:
                @pl.when(m > 0)
                def _():
                    for d in range(1, 4):
                        spread_arrived(m - 1, d).wait_recv()

                @pl.when((m > 0) & (m < 3))
                def _():
                    for way in range(2):
                        halo_copy(m - 1, way).start()
            if s == 0:
                compute(0, y, True)
            else:
                for way in range(2):
                    compute(slot(way, s - 1), place(way, s - 1))
        compute(4, place(0, 3))
        spread = acc[...].T.astype(BF16).reshape(4, 192, 128)
        proj[m] = spread
        for d in range(1, 4):
            spread_copy(m, d).start()
        recv[m, 2 + zl] = proj[m, zl]
        return 0

    lax.fori_loop(0, 4, gather_one, 0)

    for m in (KEY, VALUE):
        for way in range(2):
            halo_copy(m, way).wait_recv()
    for e in range(8):
        for m, natural, turned in ((KEY, kn, kt), (VALUE, vn, vt)):
            block = recv[m, e]
            flat = block.T
            for h in range(3):
                turned[h, :, 128 * e:128 * e + 128] = block[64 * h:64 * h + 64]
                natural[h, 128 * e:128 * e + 128, :] = flat[:, 64 * h:64 * h + 64]

    scale = HDIM ** -0.5
    dkv[...] = jnp.zeros_like(dkv)

    def window(j):
        return pl.ds(pl.multiple_of(j * 128, 128), 640)

    def head(h):
        return pl.ds(pl.multiple_of(h * 64, 64), 64)

    def forward(j, _):
        def one_head(h, _):
            scores = nn(kn[h, window(j), :], recv[QUERY, 2 + j, head(h), :]) * scale
            exps = jnp.exp(scores - jnp.max(scores, axis=0, keepdims=True))
            weights = (exps / jnp.sum(exps, axis=0, keepdims=True)).astype(BF16)
            probs[j, h] = weights
            mix[j, head(h), :] = nn(vt[h, :, window(j)], weights).astype(BF16)
            return 0

        lax.fori_loop(0, 3, one_head, 0)
        send_back(MIX, mix.at[j], j)
        return 0

    lax.fori_loop(0, 4, forward, 0)
    for d in range(1, 4):
        spread_arrived(OUT, d).wait_recv()

    def backward(j, _):
        def one_head(h, _):
            dm = recv[OUT, 2 + j, head(h), :]
            delta = jnp.sum(dm.astype(F32) * mix[j, head(h), :].astype(F32), axis=0, keepdims=True)
            weights = probs[j, h]
            d_weights = nn(vn[h, window(j), :], dm)
            d_scores = (weights.astype(F32) * (d_weights - delta) * scale).astype(BF16)
            dq[j, head(h), :] = nn(kt[h, :, window(j)], d_scores).astype(BF16)
            dkv[0, h, :, window(j)] += nt(recv[QUERY, 2 + j, head(h), :], d_scores)
            dkv[1, h, :, window(j)] += nt(dm, weights)
            return 0

        lax.fori_loop(0, 3, one_head, 0)
        send_back(DQ, dq.at[j], j)
        return 0

    lax.fori_loop(0, 2, backward, 0)
    wait_back(MIX)
    other_mix().start()
    lax.fori_loop(2, 4, backward, 0)

    for kv in (1, 0):
        for way in range(2):
            lanes = slice(0, 256) if way == 0 else slice(768, 1024)
            halo_out[kv, way] = dkv[kv, :, :, lanes].astype(BF16).reshape(192, 256)
            ghalo_copy(kv, way).start()

    other_mix().wait_recv()
    other_half().wait_recv()

    def grad_rows(d, _):
        to = (x + d) % 4
        part = nn(back[MIX, to], up_half[c]) + nn(mix_other[to], up_other[...])
        xs[to] = part.astype(BF16)

        @pl.when(d > 0)
        def _():
            x_copy(d).start()

        return 0

    lax.fori_loop(1, 5, lambda d, r: grad_rows(d % 4, r), 0)

    def natural(t):
        return back[t].reshape(768, 128).T

    mixture = natural(MIX)
    for i in range(4):
        lanes = slice(384 * i, 384 * i + 384)
        branch = nt(mixture, wall[OUT, 2 * i:2 * i + 2].reshape(384, 768))
        x_ref[0, :, lanes] = (first_ref[0, :, lanes].astype(F32) - branch).astype(BF16)

    for kv in (1, 0):
        for way in range(2):
            ghalo_copy(kv, way).wait_recv()
        for j in range(4):
            way = j // 2
            got = halo_in[kv, 1 - way, :, 128 * (j % 2):128 * (j % 2) + 128].astype(F32)
            own = dkv[kv, :, :, 256 + 128 * j:384 + 128 * j].reshape(192, 128)
            dkv_out[kv, j] = (own + got).astype(BF16)
            send_back(DK + kv, dkv_out.at[kv, j], j)

    for d in range(1, 4):
        x_copy(d).wait_recv()
    part = xs[x].astype(F32)
    for d in range(3):
        part = part + xr[d].astype(F32)
    ys[...] = part.T.astype(BF16).reshape(8, 96, 192)
    for d in range(1, 8):
        y_copy(d).start()

    def add_unit(t, m, first=False):
        wait_back(t)
        grads = natural(t)
        for i in range(4):
            lanes = slice(384 * i, 384 * i + 384)
            term = nt(grads, wall[m, 2 * i:2 * i + 2].reshape(384, 768))
            if first:
                d_unit[:, lanes] = term
            else:
                d_unit[:, lanes] += term

    add_unit(DQ, QUERY, True)
    add_unit(DV, VALUE)

    for d in range(1, 8):
        y_copy(d).wait_recv()
    part = ys[y].astype(F32)
    for d in range(7):
        part = part + yr[d].astype(F32)
    zs[...] = part.T.reshape(4, 48, 96)
    for d, other in z_partners:
        z_copy(d, other).start()

    add_unit(DK, KEY)
    values = second_ref[0].astype(F32)
    center = values - jnp.mean(values, axis=-1, keepdims=True)
    inv_std = lax.rsqrt(jnp.mean(center * center, axis=-1, keepdims=True) + EPSILON)
    unit = center * inv_std
    grads = d_unit[...]
    correction = (grads - jnp.mean(grads, axis=-1, keepdims=True)
                  - unit * jnp.mean(grads * unit, axis=-1, keepdims=True))
    dx_ref[0] = (dsecond_ref[0].astype(F32) + inv_std * correction).astype(BF16)

    for d, other in z_partners:
        z_copy(d, other).wait_recv()
    part = zs[zl]
    for n in range(7):
        part = part + zr[n]
    grad_ref[...] = jnp.where(zh == 0, part[:, :48], part[:, 48:]) / 32

    def drain(m, _):
        @pl.when(edge)
        def _():
            far_copy(m, 0).wait_send()
            near_copy(m).wait_send()

        for q in range(2):
            for way in range(2):
                for s in range(STEPS[q][way]):
                    ring_copy(m, q, way, s).wait_send()
            for j in range(8):
                core_copy(m, q, j, y, c).wait_send()
        for d in range(1, 4):
            spread_copy(m, d).wait_send()
            g = (zl + d) % 4
            back_copy(m, mix.at[g], g).wait_send()
        return 0

    lax.fori_loop(0, 4, drain, 0)
    for kv in range(2):
        for way in range(2):
            halo_copy(kv, way).wait_send()
            ghalo_copy(kv, way).wait_send()
    other_half().wait_send()
    other_mix().wait_send()
    for d in range(1, 4):
        x_copy(d).wait_send()
    for d in range(1, 8):
        y_copy(d).wait_send()
    for d, other in z_partners:
        z_copy(d, other).wait_send()


def block(y_first, y_second, upstream, dy_second, in_proj, out_t):
    vmem = pl.BlockSpec(memory_space=pltpu.VMEM)
    dma = pltpu.SemaphoreType.DMA
    stream = jax.ShapeDtypeStruct((1, 128, 1536), BF16)
    return pl.pallas_call(
        kernel,
        out_shape=(stream, stream, jax.ShapeDtypeStruct((48, 48), F32)),
        in_specs=[vmem] * 6,
        out_specs=(vmem,) * 3,
        scratch_shapes=[
            pltpu.VMEM((4, 8, 2, 2, 48, 768), BF16),
            pltpu.VMEM((2, 8, 128, 192), BF16),
            pltpu.VMEM((128, 768), F32),
            pltpu.VMEM((4, 4, 192, 128), BF16),
            pltpu.VMEM((4, 8, 192, 128), BF16),
            pltpu.VMEM((3, 1024, 64), BF16),
            pltpu.VMEM((3, 1024, 64), BF16),
            pltpu.VMEM((3, 64, 1024), BF16),
            pltpu.VMEM((3, 64, 1024), BF16),
            pltpu.VMEM((4, 3, 640, 128), BF16),
            pltpu.VMEM((4, 192, 128), BF16),
            pltpu.VMEM((4, 192, 128), BF16),
            pltpu.VMEM((2, 3, 64, 1024), F32),
            pltpu.VMEM((2, 2, 192, 256), BF16),
            pltpu.VMEM((2, 2, 192, 256), BF16),
            pltpu.VMEM((2, 4, 192, 128), BF16),
            pltpu.VMEM((4, 4, 192, 128), BF16),
            pltpu.VMEM((128, 1536), F32),
            pltpu.VMEM((2, 128, 768), BF16),
            pltpu.VMEM((128, 768), BF16),
            pltpu.VMEM((4, 192, 128), BF16),
            pltpu.VMEM((4, 192, 768), BF16),
            pltpu.VMEM((3, 192, 768), BF16),
            pltpu.VMEM((8, 96, 192), BF16),
            pltpu.VMEM((7, 96, 192), BF16),
            pltpu.VMEM((4, 48, 96), F32),
            pltpu.VMEM((7, 48, 96), F32),
            dma((4,)), dma((4,)), dma((4,)),
            dma((4, 2, 2, 4)), dma((4, 2, 2, 4)),
            dma((4, 2, 8)), dma((4, 2, 8)),
            dma((2,)), dma((2,)),
            dma((4, 3)), dma((4, 3)),
            dma((2, 2)), dma((2, 2)),
            dma((2, 2)), dma((2, 2)),
            dma((4, 4)), dma((4, 4)),
            dma((3,)), dma((3,)),
            dma((7,)), dma((7,)),
            dma((7,)), dma((7,)),
        ],
        compiler_params=pltpu.CompilerParams(
            collective_id=0, has_side_effects=True, vmem_limit_bytes=50 * 2**20),
        name="attention_block_backward",
    )(y_first, y_second, upstream, dy_second, in_proj, out_t)


def body(y_first, y_second, first_output_cotangent, dy_second, in_proj, out_proj):
    return block(y_first, y_second, first_output_cotangent, dy_second, in_proj, out_proj.T)


def solution(mesh):
    placed = (
        P("wide", "blk", None),
        P("wide", "blk", None),
        P("wide", "blk", None),
        P("wide", "blk", None),
        P(None, "wide", None),
        P(None, "wide"),
    )
    return jax.shard_map(
        body,
        mesh=mesh,
        in_specs=placed,
        out_specs=(P("wide", "blk", None), P("wide", "blk", None), P("blk", "wide")),
        check_vma=False,
    )
```

```python
import functools

import jax
import jax.numpy as jnp
from jax import lax
from jax.experimental import pallas as pl
from jax.experimental.pallas import tpu as pltpu
from jax.sharding import PartitionSpec as P

HDIM = 64
EPSILON = 1e-05
MESH = pl.DeviceIdType.MESH
F32 = jnp.float32
BF16 = jnp.bfloat16

KEY, VALUE, QUERY, OUT = range(4)
MIX, DQ, DK, DV = range(4)


def nt(a, b):
    return lax.dot_general(a, b, (((1,), (1,)), ((), ())), preferred_element_type=F32)


def nn(a, b):
    return jnp.dot(a, b, preferred_element_type=F32)


def kernel(first_ref, second_ref, upstream_ref, dsecond_ref, in_ref, out_ref,
           x_ref, dx_ref, grad_ref,
           first, second, upstream_in, dsecond, wall, lhs, acc, proj, recv, kn, vn, kt, vt, probs, mix, dq, dkv, halo_out,
           halo_in, dkv_out, back, d_unit, up_half, up_other, mix_other, xs, xr, ys, yr, zs, zr,
           load_sem, stream_sem, far_send, near_send, far_recv, ring_send, ring_recv,
           cross_send, cross_recv, core_send, core_recv,
           swap_send, swap_recv, spread_send, spread_recv, halo_send, halo_recv,
           ghalo_send, ghalo_recv, back_send, back_recv,
           xs_send, xs_recv, ys_send, ys_recv, zs_send, zs_recv):
    b, w = lax.axis_index("blk"), lax.axis_index("wide")
    x, zl, y, zh, c = b // 4, b % 4, w // 4, (w // 2) % 2, w % 2
    edge = (zl == 0) | (zl == 3)
    half = (zh, 1 - zh)
    carried, parity = (zh + c) % 2, x % 2

    def at_x(d):
        return {"blk": ((x + d) % 4) * 4 + zl}

    def at_y(d):
        return {"wide": ((y + d) % 8) * 4 + zh * 2 + c}

    def at_z(d, other):
        return {"blk": x * 4 + (zl + d) % 4, "wide": w + other * (2 - 4 * zh)}

    above, below = at_y(1), at_y(7)
    partner = {"wide": w + 1 - 2 * c}
    far = {"blk": b + 3 - 2 * zl, "wide": w + 2 - 4 * zh}
    near = {"blk": b + 1 - 2 * (b % 2)}

    def copy(src, dst, send, got, device):
        return pltpu.make_async_remote_copy(
            src_ref=src, dst_ref=dst, send_sem=send, recv_sem=got,
            device_id=device, device_id_type=MESH)

    barrier = pltpu.get_barrier_semaphore()
    greeted = [partner] + [at_x(d) for d in range(1, 4)] + [at_y(d) for d in range(1, 8)]
    greeted += [at_z(d, 0) for d in range(1, 4)] + [at_z(d, 1) for d in range(4)]
    for device in greeted:
        pl.semaphore_signal(barrier, inc=1, device_id=device, device_id_type=MESH)

    def load_weight(m):
        source = (in_ref.at[1], in_ref.at[2], in_ref.at[0], out_ref)[m]
        return pltpu.make_async_copy(source, wall.at[m, y, zh, c], load_sem.at[m])

    streams = ((second_ref, second), (upstream_ref, upstream_in), (first_ref, first),
               (dsecond_ref, dsecond))

    def load_stream(i):
        return pltpu.make_async_copy(streams[i][0].at[0], streams[i][1], stream_sem.at[i])

    for m in range(4):
        load_weight(m).start()
    for i in range(4):
        load_stream(i).start()
    for m in range(4):
        load_weight(m).wait()
    pl.semaphore_wait(barrier, len(greeted))

    def far_copy(m, q):
        block = wall.at[m, y, half[q], c]
        return copy(block, block, far_send.at[m], far_recv.at[m], far)

    def near_copy(m):
        block = wall.at[m, y, half[1], c]
        return copy(block, block, near_send.at[m], far_recv.at[m], near)

    def place(way, s):
        return (y + 7 - s) % 8 if way == 0 else (y + 1 + s) % 8

    def slot(way, s):
        return s if way == 0 else 4 + s

    def ring_copy(m, way, s):
        origin = (y + 8 - s) % 8 if way == 0 else (y + s) % 8
        block = wall.at[m, origin, carried, parity]
        j = slot(way, s)
        return copy(block, block, ring_send.at[m, j], ring_recv.at[m, j],
                    above if way == 0 else below)

    def ring_got(m, way, s):
        block = wall.at[m, place(way, s), carried, parity]
        j = slot(way, s)
        return copy(block, block, ring_send.at[m, j], ring_recv.at[m, j], above)

    def ring_last(m):
        block = wall.at[m, (y + 5 + 6 * c) % 8, carried, parity]
        return copy(block, block, ring_send.at[m, 3], ring_recv.at[m, 3],
                    {"wide": ((y + 1 + 6 * c) % 8) * 4 + zh * 2 + c})

    def cross_copy(m, way, s):
        block = wall.at[m, place(way, s), carried, parity]
        j = slot(way, s)
        to = 1 + 2 * c if s == 3 else (1, 3)[way]
        return copy(block, block, cross_send.at[m, j], cross_recv.at[m, j], at_x(to))

    def cross_got(m, way, s):
        block = wall.at[m, place(way, s), carried, 1 - parity]
        j = slot(way, s)
        return copy(block, block, cross_send.at[m, j], cross_recv.at[m, j], at_x(1))

    def core_copy(m, kind, way, s, mine=True):
        half_of = carried if mine else 1 - carried
        block = wall.at[m, place(way, s), half_of, 1 - parity if kind else parity]
        j = slot(way, s)
        return copy(block, block, core_send.at[m, kind, j], core_recv.at[m, kind, j], partner)

    def core_own(m, kind, core):
        block = wall.at[m, y, half[kind], core]
        return copy(block, block, core_send.at[m, kind, 7], core_recv.at[m, kind, 7], partner)

    def ways_of(s):
        return (0, 1) if s < 3 else (0,)

    def start_stream(m):
        for way in range(2):
            ring_copy(m, way, 0).start()

    def have_own(m):
        core_own(m, 0, 1 - c).wait_recv()

        @pl.when(c == 0)
        def _():
            start_stream(m)

    def pass_far(m):
        far_copy(m, 1).wait_recv()

        @pl.when(edge)
        def _():
            near_copy(m).start()

        core_own(m, 1, c).start()

    def have_far(m):
        core_own(m, 1, 1 - c).wait_recv()

        @pl.when(c == 1)
        def _():
            start_stream(m)

    def ring_step(m, s):
        for way in ways_of(s):
            ring_got(m, way, s).wait_recv()
            if s < 2:
                ring_copy(m, way, s + 1).start()
            if s == 2:
                @pl.when(c == way)
                def _():
                    ring_last(m).start()
            cross_copy(m, way, s).start()
            core_copy(m, 0, way, s).start()

    def cross_step(m, s):
        for way in ways_of(s):
            cross_got(m, way, s).wait_recv()
            core_copy(m, 1, way, s).start()

    def project(m, origin, first=False):
        term = nn(lhs[m // 3, origin], wall[m, origin].reshape(192, 768))
        if first:
            acc[m] = term
        else:
            acc[m] += term

    def project_step(m, s):
        for way in ways_of(s):
            for kind in range(2):
                core_copy(m, kind, way, s, False).wait_recv()
            project(m, place(way, s))

    def spread_copy(m, d):
        return copy(proj.at[m, (zl + d) % 4], recv.at[m, 2 + zl], spread_send.at[m, d - 1],
                    spread_recv.at[m, d - 1], at_z(d, 0))

    def spread_arrived(m, d):
        return copy(proj.at[m, (zl + d) % 4], recv.at[m, 2 + (zl + 4 - d) % 4],
                    spread_send.at[m, d - 1], spread_recv.at[m, d - 1], at_z(d, 0))

    def halo_copy(m, way, arriving=False):
        start = (4, 2)[way]
        into = (0, 6)[way]
        return copy(recv.at[m, start:start + 2], recv.at[m, into:into + 2],
                    halo_send.at[m, way], halo_recv.at[m, way], at_x((1, 3)[way]))

    def ghalo_copy(kv, way):
        return copy(halo_out.at[kv, way], halo_in.at[kv, way], ghalo_send.at[kv, way],
                    ghalo_recv.at[kv, way], at_x((3, 1)[way]))

    def back_copy(t, source, j):
        return copy(source, back.at[t, zl], back_send.at[t, j], back_recv.at[t, zl],
                    {"blk": x * 4 + j})

    def send_back(t, source, j):
        @pl.when(j != zl)
        def _():
            back_copy(t, source, j).start()

        @pl.when(j == zl)
        def _():
            back[t, zl] = source[...]

    def wait_back(t):
        for d in range(1, 4):
            g = (zl + d) % 4
            copy(back.at[t, g], back.at[t, g], back_send.at[t, g], back_recv.at[t, g],
                 {"blk": x * 4 + g}).wait_recv()

    def other_half():
        return copy(up_half.at[1 - c], up_other, swap_send.at[0], swap_recv.at[0], partner)

    def other_mix():
        return copy(back.at[MIX], mix_other, swap_send.at[1], swap_recv.at[1], partner)

    def x_copy(d):
        return copy(xs.at[(x + d) % 4], xr.at[d - 1], xs_send.at[d - 1], xs_recv.at[d - 1], at_x(d))

    def y_copy(d):
        return copy(ys.at[(y + d) % 8], yr.at[d - 1], ys_send.at[d - 1], ys_recv.at[d - 1], at_y(d))

    def z_copy(d, other):
        n = d + 4 * other - 1
        return copy(zs.at[(zl + d) % 4], zr.at[n], zs_send.at[n], zs_recv.at[n], at_z(d, other))

    z_partners = [(d, 0) for d in range(1, 4)] + [(d, 1) for d in range(4)]

    @pl.when(edge)
    def _():
        for m in range(4):
            far_copy(m, 0).start()

    for m in range(4):
        core_own(m, 0, c).start()
    for m in range(2):
        have_own(m)

    load_stream(0).wait()
    values = second[...].astype(F32)
    center = values - jnp.mean(values, axis=-1, keepdims=True)
    inv_std = lax.rsqrt(jnp.mean(center * center, axis=-1, keepdims=True) + EPSILON)
    unit_b = (center * inv_std).astype(BF16)
    load_stream(1).wait()
    upstream = upstream_in[...]
    for i in range(8):
        lhs[0, i] = unit_b[:, 192 * i:192 * i + 192]
        lhs[1, i] = upstream[:, 192 * i:192 * i + 192]

    for m in range(2):
        pass_far(m)
    for m in range(2):
        have_far(m)

    by_core = upstream.T.reshape(16, 2, 48, 128)
    for core in range(2):
        up_half[core] = by_core[:, core].reshape(768, 128).T
    other_half().start()

    def finish(m):
        proj[m] = acc[m].T.astype(BF16).reshape(4, 192, 128)
        for d in range(1, 4):
            spread_copy(m, d).start()
        recv[m, 2 + zl] = proj[m, zl]

    def gather_pair(g, _):
        pair = (2 * g, 2 * g + 1)
        before = (2 * g - 2, 2 * g - 1)

        def current(f, s):
            @pl.when(g < 2)
            def _():
                for m in pair:
                    f(m, s)

        def previous(f, s):
            @pl.when(g > 0)
            def _():
                for m in before:
                    f(m, s)

        previous(ring_step, 3)
        current(ring_step, 0)
        previous(cross_step, 2)
        previous(project_step, 1)

        current(ring_step, 1)
        previous(cross_step, 3)
        current(cross_step, 0)
        current(lambda m, s: project(m, y, True), 0)
        previous(project_step, 2)

        @pl.when(g == 0)
        def _():
            for m in (QUERY, OUT):
                pass_far(m)

        @pl.when(g == 2)
        def _():
            for m in (KEY, VALUE):
                for d in range(1, 4):
                    spread_arrived(m, d).wait_recv()
                for way in range(2):
                    halo_copy(m, way).start()

        current(ring_step, 2)

        @pl.when(g == 0)
        def _():
            for m in (QUERY, OUT):
                have_own(m)
            for m in (QUERY, OUT):
                have_far(m)

        current(cross_step, 1)
        previous(project_step, 3)

        @pl.when(g > 0)
        def _():
            for m in before:
                finish(m)

        current(project_step, 0)
        return 0

    lax.fori_loop(0, 3, gather_pair, 0)
    for d in range(1, 4):
        spread_arrived(QUERY, d).wait_recv()

    for m in (KEY, VALUE):
        for way in range(2):
            halo_copy(m, way).wait_recv()
    for e in range(8):
        for m, natural, turned in ((KEY, kn, kt), (VALUE, vn, vt)):
            block = recv[m, e]
            flat = block.T
            for h in range(3):
                turned[h, :, 128 * e:128 * e + 128] = block[64 * h:64 * h + 64]
                natural[h, 128 * e:128 * e + 128, :] = flat[:, 64 * h:64 * h + 64]

    scale = HDIM ** -0.5
    dkv[...] = jnp.zeros_like(dkv)

    def window(j):
        return pl.ds(pl.multiple_of(j * 128, 128), 640)

    def head(h):
        return pl.ds(pl.multiple_of(h * 64, 64), 64)

    def forward(j, _):
        def one_head(h, _):
            scores = nn(kn[h, window(j), :], recv[QUERY, 2 + j, head(h), :]) * scale
            exps = jnp.exp(scores - jnp.max(scores, axis=0, keepdims=True))
            weights = (exps / jnp.sum(exps, axis=0, keepdims=True)).astype(BF16)
            probs[j, h] = weights
            mix[j, head(h), :] = nn(vt[h, :, window(j)], weights).astype(BF16)
            return 0

        lax.fori_loop(0, 3, one_head, 0)
        send_back(MIX, mix.at[j], j)
        return 0

    lax.fori_loop(0, 4, forward, 0)
    for d in range(1, 4):
        spread_arrived(OUT, d).wait_recv()

    def backward(j, _):
        def one_head(h, _):
            dm = recv[OUT, 2 + j, head(h), :]
            delta = jnp.sum(dm.astype(F32) * mix[j, head(h), :].astype(F32), axis=0, keepdims=True)
            weights = probs[j, h]
            d_weights = nn(vn[h, window(j), :], dm)
            d_scores = (weights.astype(F32) * (d_weights - delta) * scale).astype(BF16)
            dq[j, head(h), :] = nn(kt[h, :, window(j)], d_scores).astype(BF16)
            dkv[0, h, :, window(j)] += nt(recv[QUERY, 2 + j, head(h), :], d_scores)
            dkv[1, h, :, window(j)] += nt(dm, weights)
            return 0

        lax.fori_loop(0, 3, one_head, 0)
        send_back(DQ, dq.at[j], j)
        return 0

    lax.fori_loop(0, 2, backward, 0)
    wait_back(MIX)
    other_mix().start()
    lax.fori_loop(2, 4, backward, 0)

    for kv in (1, 0):
        for way in range(2):
            lanes = slice(0, 256) if way == 0 else slice(768, 1024)
            halo_out[kv, way] = dkv[kv, :, :, lanes].astype(BF16).reshape(192, 256)
            ghalo_copy(kv, way).start()

    other_mix().wait_recv()
    other_half().wait_recv()

    def grad_rows(d, _):
        to = (x + d) % 4
        part = nn(back[MIX, to], up_half[c]) + nn(mix_other[to], up_other[...])
        xs[to] = part.astype(BF16)

        @pl.when(d > 0)
        def _():
            x_copy(d).start()

        return 0

    lax.fori_loop(1, 5, lambda d, r: grad_rows(d % 4, r), 0)

    def natural(t):
        return back[t].reshape(768, 128).T

    load_stream(2).wait()
    mixture = natural(MIX)
    for i in range(4):
        lanes = slice(384 * i, 384 * i + 384)
        branch = nt(mixture, wall[OUT, 2 * i:2 * i + 2].reshape(384, 768))
        x_ref[0, :, lanes] = (first[:, lanes].astype(F32) - branch).astype(BF16)

    for kv in (1, 0):
        for way in range(2):
            ghalo_copy(kv, way).wait_recv()
        for j in range(4):
            way = j // 2
            got = halo_in[kv, 1 - way, :, 128 * (j % 2):128 * (j % 2) + 128].astype(F32)
            own = dkv[kv, :, :, 256 + 128 * j:384 + 128 * j].reshape(192, 128)
            dkv_out[kv, j] = (own + got).astype(BF16)
            send_back(DK + kv, dkv_out.at[kv, j], j)

    for d in range(1, 4):
        x_copy(d).wait_recv()
    part = xs[x].astype(F32)
    for d in range(3):
        part = part + xr[d].astype(F32)
    ys[...] = part.T.astype(BF16).reshape(8, 96, 192)
    for d in range(1, 8):
        y_copy(d).start()

    def add_unit(t, m, first=False):
        wait_back(t)
        grads = natural(t)
        for i in range(4):
            lanes = slice(384 * i, 384 * i + 384)
            term = nt(grads, wall[m, 2 * i:2 * i + 2].reshape(384, 768))
            if first:
                d_unit[:, lanes] = term
            else:
                d_unit[:, lanes] += term

    add_unit(DQ, QUERY, True)
    add_unit(DV, VALUE)

    for d in range(1, 8):
        y_copy(d).wait_recv()
    part = ys[y].astype(F32)
    for d in range(7):
        part = part + yr[d].astype(F32)
    zs[...] = part.T.reshape(4, 48, 96)
    for d, other in z_partners:
        z_copy(d, other).start()

    add_unit(DK, KEY)
    values = second[...].astype(F32)
    center = values - jnp.mean(values, axis=-1, keepdims=True)
    inv_std = lax.rsqrt(jnp.mean(center * center, axis=-1, keepdims=True) + EPSILON)
    unit = center * inv_std
    grads = d_unit[...]
    correction = (grads - jnp.mean(grads, axis=-1, keepdims=True)
                  - unit * jnp.mean(grads * unit, axis=-1, keepdims=True))
    load_stream(3).wait()
    dx_ref[0] = (dsecond[...].astype(F32) + inv_std * correction).astype(BF16)

    for d, other in z_partners:
        z_copy(d, other).wait_recv()
    part = zs[zl]
    for n in range(7):
        part = part + zr[n]
    grad_ref[...] = jnp.where(zh == 0, part[:, :48], part[:, 48:]) / 32

    def drain(m, _):
        @pl.when(edge)
        def _():
            far_copy(m, 0).wait_send()
            near_copy(m).wait_send()

        for s in range(4):
            for way in ways_of(s):
                if s < 3:
                    ring_copy(m, way, s).wait_send()
                else:
                    ring_last(m).wait_send()
                cross_copy(m, way, s).wait_send()
                for kind in range(2):
                    core_copy(m, kind, way, s).wait_send()
        for kind in range(2):
            core_own(m, kind, c).wait_send()
        for d in range(1, 4):
            spread_copy(m, d).wait_send()
            g = (zl + d) % 4
            back_copy(m, mix.at[g], g).wait_send()
        return 0

    lax.fori_loop(0, 4, drain, 0)
    for kv in range(2):
        for way in range(2):
            halo_copy(kv, way).wait_send()
            ghalo_copy(kv, way).wait_send()
    other_half().wait_send()
    other_mix().wait_send()
    for d in range(1, 4):
        x_copy(d).wait_send()
    for d in range(1, 8):
        y_copy(d).wait_send()
    for d, other in z_partners:
        z_copy(d, other).wait_send()


def block(y_first, y_second, upstream, dy_second, in_proj, out_t):
    vmem = pl.BlockSpec(memory_space=pltpu.VMEM)
    dma = pltpu.SemaphoreType.DMA
    stream = jax.ShapeDtypeStruct((1, 128, 1536), BF16)
    return pl.pallas_call(
        kernel,
        out_shape=(stream, stream, jax.ShapeDtypeStruct((48, 48), F32)),
        in_specs=[pl.BlockSpec(memory_space=pl.ANY)] * 6,
        out_specs=(vmem,) * 3,
        scratch_shapes=[
            pltpu.VMEM((128, 1536), BF16),
            pltpu.VMEM((128, 1536), BF16),
            pltpu.VMEM((128, 1536), BF16),
            pltpu.VMEM((128, 1536), BF16),
            pltpu.VMEM((4, 8, 2, 2, 48, 768), BF16),
            pltpu.VMEM((2, 8, 128, 192), BF16),
            pltpu.VMEM((4, 128, 768), F32),
            pltpu.VMEM((4, 4, 192, 128), BF16),
            pltpu.VMEM((4, 8, 192, 128), BF16),
            pltpu.VMEM((3, 1024, 64), BF16),
            pltpu.VMEM((3, 1024, 64), BF16),
            pltpu.VMEM((3, 64, 1024), BF16),
            pltpu.VMEM((3, 64, 1024), BF16),
            pltpu.VMEM((4, 3, 640, 128), BF16),
            pltpu.VMEM((4, 192, 128), BF16),
            pltpu.VMEM((4, 192, 128), BF16),
            pltpu.VMEM((2, 3, 64, 1024), F32),
            pltpu.VMEM((2, 2, 192, 256), BF16),
            pltpu.VMEM((2, 2, 192, 256), BF16),
            pltpu.VMEM((2, 4, 192, 128), BF16),
            pltpu.VMEM((4, 4, 192, 128), BF16),
            pltpu.VMEM((128, 1536), F32),
            pltpu.VMEM((2, 128, 768), BF16),
            pltpu.VMEM((128, 768), BF16),
            pltpu.VMEM((4, 192, 128), BF16),
            pltpu.VMEM((4, 192, 768), BF16),
            pltpu.VMEM((3, 192, 768), BF16),
            pltpu.VMEM((8, 96, 192), BF16),
            pltpu.VMEM((7, 96, 192), BF16),
            pltpu.VMEM((4, 48, 96), F32),
            pltpu.VMEM((7, 48, 96), F32),
            dma((4,)), dma((4,)),
            dma((4,)), dma((4,)), dma((4,)),
            dma((4, 7)), dma((4, 7)),
            dma((4, 7)), dma((4, 7)),
            dma((4, 2, 8)), dma((4, 2, 8)),
            dma((2,)), dma((2,)),
            dma((4, 3)), dma((4, 3)),
            dma((2, 2)), dma((2, 2)),
            dma((2, 2)), dma((2, 2)),
            dma((4, 4)), dma((4, 4)),
            dma((3,)), dma((3,)),
            dma((7,)), dma((7,)),
            dma((7,)), dma((7,)),
        ],
        compiler_params=pltpu.CompilerParams(
            collective_id=0, has_side_effects=True, vmem_limit_bytes=62 * 2**20),
        name="attention_block_backward",
    )(y_first, y_second, upstream, dy_second, in_proj, out_t)


def body(y_first, y_second, first_output_cotangent, dy_second, in_proj, out_proj):
    return block(y_first, y_second, first_output_cotangent, dy_second, in_proj, out_proj.T)


def solution(mesh):
    placed = (
        P("wide", "blk", None),
        P("wide", "blk", None),
        P("wide", "blk", None),
        P("wide", "blk", None),
        P(None, "wide", None),
        P(None, "wide"),
    )
    return jax.shard_map(
        body,
        mesh=mesh,
        in_specs=placed,
        out_specs=(P("wide", "blk", None), P("wide", "blk", None), P("blk", "wide")),
        check_vma=False,
    )
```

```python
import functools

import jax
import jax.numpy as jnp
from jax import lax
from jax.experimental import pallas as pl
from jax.experimental.pallas import tpu as pltpu
from jax.sharding import PartitionSpec as P

HDIM = 64
EPSILON = 1e-05
MESH = pl.DeviceIdType.MESH
F32 = jnp.float32
BF16 = jnp.bfloat16

KEY, VALUE, QUERY, OUT = range(4)
MIX, DQ, DK, DV = range(4)


def nt(a, b):
    return lax.dot_general(a, b, (((1,), (1,)), ((), ())), preferred_element_type=F32)


def nn(a, b):
    return jnp.dot(a, b, preferred_element_type=F32)


def kernel(first_ref, second_ref, upstream_ref, dsecond_ref, in_ref, out_ref,
           x_ref, dx_ref, grad_ref,
           first, second, upstream_in, dsecond, wall, lhs, acc, proj, recv, kn, vn, kt, vt, probs, mix, dq, dkv, halo_out,
           halo_in, dkv_out, back, d_unit, up_all, up_other, mix_other, dm_all, dm, xs, xr, ys, yr,
           fs, fr,
           load_sem, stream_sem, far_send, near_send, far_recv, ring_send, ring_recv,
           cross_send, cross_recv, core_send, core_recv,
           line_send, line_recv, swap_send, swap_recv, spread_send, spread_recv, halo_send, halo_recv,
           ghalo_send, ghalo_recv, back_send, back_recv,
           xs_send, xs_recv, ys_send, ys_recv, fs_send, fs_recv):
    b, w = lax.axis_index("blk"), lax.axis_index("wide")
    x, zl, y, zh, c = b // 4, b % 4, w // 4, (w // 2) % 2, w % 2
    edge = (zl == 0) | (zl == 3)
    half = (zh, 1 - zh)
    carried, parity = (zh + c) % 2, x % 2

    def at_x(d):
        return {"blk": ((x + d) % 4) * 4 + zl}

    def at_y(d):
        return {"wide": ((y + d) % 8) * 4 + zh * 2 + c}

    def at_z(d):
        return {"blk": x * 4 + (zl + d) % 4}

    above, below = at_y(1), at_y(7)
    partner = {"wide": w + 1 - 2 * c}
    crosses = edge & ((parity == 0) | (c == 1))
    far = {"blk": b + 3 - 2 * zl,
           "wide": y * 4 + (1 - zh) * 2 + jnp.where(parity == 0, 1 - c, c)}
    near = {"blk": b + 1 - 2 * (b % 2)}

    def copy(src, dst, send, got, device):
        return pltpu.make_async_remote_copy(
            src_ref=src, dst_ref=dst, send_sem=send, recv_sem=got,
            device_id=device, device_id_type=MESH)

    barrier = pltpu.get_barrier_semaphore()
    greeted = [partner] + [at_x(d) for d in range(1, 4)] + [at_y(d) for d in range(1, 8)]
    greeted += [at_z(d) for d in range(1, 4)]
    turned_here = {"blk": zl * 4 + x}
    turned_far = {"blk": zl * 4 + x, "wide": w + 2 - 4 * zh}
    for device in greeted:
        pl.semaphore_signal(barrier, inc=1, device_id=device, device_id_type=MESH)

    @pl.when(crosses)
    def _():
        pl.semaphore_signal(barrier, inc=1, device_id=far, device_id_type=MESH)

    pl.semaphore_signal(barrier, inc=1, device_id=turned_far, device_id_type=MESH)

    @pl.when(x != zl)
    def _():
        pl.semaphore_signal(barrier, inc=1, device_id=turned_here, device_id_type=MESH)

    def load_weight(m):
        source = (in_ref.at[1], in_ref.at[2], in_ref.at[0], out_ref)[m]
        return pltpu.make_async_copy(source, wall.at[m, y, zh, c], load_sem.at[m])

    streams = ((second_ref, second), (upstream_ref, upstream_in), (first_ref, first),
               (dsecond_ref, dsecond))

    def load_stream(i):
        return pltpu.make_async_copy(streams[i][0].at[0], streams[i][1], stream_sem.at[i])

    for m in range(4):
        load_weight(m).start()
    for i in range(4):
        load_stream(i).start()
    for m in range(4):
        load_weight(m).wait()
    extra = 1 + crosses.astype(jnp.int32) + (x != zl).astype(jnp.int32)
    pl.semaphore_wait(barrier, len(greeted) + extra)

    def far_copy(m):
        block = wall.at[m, y, zh, c]
        return copy(block, block, far_send.at[m], far_recv.at[m], far)

    def near_copy(m):
        block = wall.at[m, y, 1 - zh, parity]
        return copy(block, block, near_send.at[m], far_recv.at[m], near)

    def place(way, s):
        return (y + 7 - s) % 8 if way == 0 else (y + 1 + s) % 8

    def slot(way, s):
        return s if way == 0 else 4 + s

    def ring_copy(m, way, s):
        origin = (y + 8 - s) % 8 if way == 0 else (y + s) % 8
        block = wall.at[m, origin, carried, parity]
        j = slot(way, s)
        return copy(block, block, ring_send.at[m, j], ring_recv.at[m, j],
                    above if way == 0 else below)

    def ring_got(m, way, s):
        block = wall.at[m, place(way, s), carried, parity]
        j = slot(way, s)
        return copy(block, block, ring_send.at[m, j], ring_recv.at[m, j], above)

    def ring_last(m):
        block = wall.at[m, (y + 5 + 6 * c) % 8, carried, parity]
        return copy(block, block, ring_send.at[m, 3], ring_recv.at[m, 3],
                    {"wide": ((y + 1 + 6 * c) % 8) * 4 + zh * 2 + c})

    def cross_copy(m, way, s):
        block = wall.at[m, place(way, s), carried, parity]
        j = slot(way, s)
        to = 1 + 2 * c if s == 3 else (1, 3)[way]
        return copy(block, block, cross_send.at[m, j], cross_recv.at[m, j], at_x(to))

    def cross_got(m, way, s):
        block = wall.at[m, place(way, s), carried, 1 - parity]
        j = slot(way, s)
        return copy(block, block, cross_send.at[m, j], cross_recv.at[m, j], at_x(1))

    def core_copy(m, kind, way, s, mine=True):
        half_of = carried if mine else 1 - carried
        block = wall.at[m, place(way, s), half_of, 1 - parity if kind else parity]
        j = slot(way, s)
        return copy(block, block, core_send.at[m, kind, j], core_recv.at[m, kind, j], partner)

    def core_own(m, core):
        block = wall.at[m, y, zh, core]
        return copy(block, block, core_send.at[m, 0, 7], core_recv.at[m, 0, 7], partner)

    def core_far(m, kind):
        block = wall.at[m, y, 1 - zh, 1 - parity if kind else parity]
        return copy(block, block, core_send.at[m, 1, 7 + kind], core_recv.at[m, 1, 7 + kind],
                    partner)

    def cross_far(m, own=True):
        block = wall.at[m, y, 1 - zh, parity if own else 1 - parity]
        return copy(block, block, cross_send.at[m, 7], cross_recv.at[m, 7], at_x(1))

    def ways_of(s):
        return (0, 1) if s < 3 else (0,)

    def start_stream(m):
        for way in range(2):
            ring_copy(m, way, 0).start()

    def have_own(m):
        core_own(m, 1 - c).wait_recv()

        @pl.when(c == 0)
        def _():
            start_stream(m)

    def begin_far(m):
        start_stream(m)
        core_far(m, 0).start()
        cross_far(m).start()

    def inner_far(m):
        @pl.when((c == 1) & jnp.logical_not(edge))
        def _():
            near_copy(m).wait_recv()

    def have_far(m):
        @pl.when(c == 1)
        def _():
            cross_far(m, False).wait_recv()
            core_far(m, 1).start()

        @pl.when(c == 0)
        def _():
            core_far(m, 0).wait_recv()
            core_far(m, 1).wait_recv()

    def ring_step(m, s):
        for way in ways_of(s):
            ring_got(m, way, s).wait_recv()
            if s < 2:
                ring_copy(m, way, s + 1).start()
            if s == 2:
                @pl.when(c == way)
                def _():
                    ring_last(m).start()
            cross_copy(m, way, s).start()
            core_copy(m, 0, way, s).start()

    def cross_step(m, s):
        for way in ways_of(s):
            cross_got(m, way, s).wait_recv()
            core_copy(m, 1, way, s).start()

    def project(m, origin, first=False):
        term = nn(lhs[origin], wall[m, origin].reshape(192, 768))
        if first:
            acc[m] = term
        else:
            acc[m] += term

    def project_step(m, s):
        for way in ways_of(s):
            for kind in range(2):
                core_copy(m, kind, way, s, False).wait_recv()

            @pl.when(m < OUT)
            def _():
                project(m, place(way, s))

    def spread_copy(m, d):
        return copy(proj.at[m, (zl + d) % 4], recv.at[m, 2 + zl], spread_send.at[m, d - 1],
                    spread_recv.at[m, d - 1], at_z(d))

    def spread_arrived(m, d):
        return copy(proj.at[m, (zl + d) % 4], recv.at[m, 2 + (zl + 4 - d) % 4],
                    spread_send.at[m, d - 1], spread_recv.at[m, d - 1], at_z(d))

    def halo_copy(m, way, arriving=False):
        start = (4, 2)[way]
        into = (0, 6)[way]
        return copy(recv.at[m, start:start + 2], recv.at[m, into:into + 2],
                    halo_send.at[m, way], halo_recv.at[m, way], at_x((1, 3)[way]))

    def ghalo_copy(kv, way):
        return copy(halo_out.at[kv, way], halo_in.at[kv, way], ghalo_send.at[kv, way],
                    ghalo_recv.at[kv, way], at_x((3, 1)[way]))

    def back_copy(t, source, j):
        return copy(source, back.at[t, zl], back_send.at[t, j], back_recv.at[t, zl],
                    {"blk": x * 4 + j})

    def send_back(t, source, j):
        @pl.when(j != zl)
        def _():
            back_copy(t, source, j).start()

        @pl.when(j == zl)
        def _():
            back[t, zl] = source[...]

    def wait_back(t):
        for d in range(1, 4):
            g = (zl + d) % 4
            copy(back.at[t, g], back.at[t, g], back_send.at[t, g], back_recv.at[t, g],
                 {"blk": x * 4 + g}).wait_recv()

    def line_sends(way, k):
        return (zl < 3) & (zl >= k) if way == 0 else (zl > 0) & (zl + k <= 3)

    def line_gets(way, k):
        return zl >= k + 1 if way == 0 else zl + k <= 2

    def line_copy(way, k, part):
        block = up_all.at[zl - k if way == 0 else zl + k, part]
        return copy(block, block, line_send.at[way, k, part], line_recv.at[way, k, part],
                    {"blk": b + 1 if way == 0 else b - 1})

    def line_got(way, k, part):
        block = up_all.at[zl - 1 - k if way == 0 else zl + 1 + k, part]
        return copy(block, block, line_send.at[way, k, part], line_recv.at[way, k, part],
                    {"blk": b + 1 if way == 0 else b - 1})

    def line_step(k, part):
        for way in range(2):
            @pl.when(line_gets(way, k))
            def _():
                line_got(way, k, part).wait_recv()

                @pl.when(line_sends(way, k + 1))
                def _():
                    line_copy(way, k + 1, part).start()

    def other_half():
        return copy(up_all.at[:, 1 - c], up_other, swap_send.at[0], swap_recv.at[0], partner)

    def other_mix():
        return copy(mix, mix_other, swap_send.at[1], swap_recv.at[1], partner)

    def x_copy(d):
        return copy(xs.at[(x + d) % 4], xr.at[d - 1], xs_send.at[d - 1], xs_recv.at[d - 1], at_x(d))

    def y_copy(d):
        return copy(ys.at[(y + d) % 8], yr.at[d - 1], ys_send.at[d - 1], ys_recv.at[d - 1], at_y(d))

    def here_copy():
        return copy(fs.at[zh], fr.at[0], fs_send.at[0], fs_recv.at[0], turned_here)

    def far_piece():
        return copy(fs.at[1 - zh], fr.at[1], fs_send.at[1], fs_recv.at[1], turned_far)

    @pl.when(edge & (c == parity))
    def _():
        for m in range(4):
            far_copy(m).start()

    for m in range(4):
        core_own(m, c).start()
    have_own(0)

    @pl.when(edge & (c == 1))
    def _():
        for m in range(4):
            near_copy(m).wait_recv()
            near_copy(m).start()
            if m == 0:
                begin_far(0)

    load_stream(1).wait()
    by_core = upstream_in[...].T.reshape(16, 2, 48, 128)
    for core in range(2):
        up_all[zl, core] = by_core[:, core].reshape(768, 128).T
    for part in range(2):
        for way in range(2):
            @pl.when(line_sends(way, 0))
            def _():
                line_copy(way, 0, part).start()

    load_stream(0).wait()
    values = second[...].astype(F32)
    center = values - jnp.mean(values, axis=-1, keepdims=True)
    inv_std = lax.rsqrt(jnp.mean(center * center, axis=-1, keepdims=True) + EPSILON)
    unit_b = (center * inv_std).astype(BF16)
    for i in range(8):
        lhs[i] = unit_b[:, 192 * i:192 * i + 192]

    @pl.when((c == 1) & jnp.logical_not(edge))
    def _():
        near_copy(0).wait_recv()
        begin_far(0)

    def finish(m):
        proj[m] = acc[m].T.astype(BF16).reshape(4, 192, 128)
        for d in range(1, 4):
            spread_copy(m, d).start()
        recv[m, 2 + zl] = proj[m, zl]

    def gather_step(t, _):
        def at(late, f, s, last=OUT):
            m = t - late - s

            @pl.when((m >= 0) & (m <= last))
            def _():
                f(m, s)

        for s in (3, 2, 1, 0):
            at(0, ring_step, s)

        @pl.when(t < 3)
        def _():
            have_own(t + 1)
            inner_far(t + 1)

            @pl.when(c == 1)
            def _():
                begin_far(t + 1)

        @pl.when(t < 6)
        def _():
            line_step(t // 2, t % 2)

        for s in (3, 2, 1, 0):
            at(1, cross_step, s)
        at(1, lambda m, s: have_far(m), 0)
        at(1, lambda m, s: project(m, y, True), 0, QUERY)
        for s in (3, 2, 1, 0):
            at(2, project_step, s)
        at(5, lambda m, s: finish(m), 0, QUERY)

        @pl.when(t == 6)
        def _():
            other_half().start()

        @pl.when(t >= 7)
        def _():
            m = t - 7
            for d in range(1, 4):
                spread_arrived(m, d).wait_recv()
            for way in range(2):
                halo_copy(m, way).start()

        return 0

    lax.fori_loop(0, 9, gather_step, 0)

    for j in range(4):
        dm_all[:, 128 * j:128 * j + 128] = sum(
            nn(up_all[j, core], wall[OUT, :, :, core].reshape(768, 768)) for core in range(2)
        ).T.astype(BF16)
    dm[...] = dm_all[pl.ds(pl.multiple_of(zl * 192, 64), 192), :]

    for m in (KEY, VALUE):
        for way in range(2):
            halo_copy(m, way).wait_recv()
    for e in range(8):
        for m, natural, turned in ((KEY, kn, kt), (VALUE, vn, vt)):
            block = recv[m, e]
            flat = block.T
            for h in range(3):
                turned[h, :, 128 * e:128 * e + 128] = block[64 * h:64 * h + 64]
                natural[h, 128 * e:128 * e + 128, :] = flat[:, 64 * h:64 * h + 64]

    for d in range(1, 4):
        spread_arrived(QUERY, d).wait_recv()
    scale = HDIM ** -0.5
    dkv[...] = jnp.zeros_like(dkv)

    def window(j):
        return pl.ds(pl.multiple_of(j * 128, 128), 640)

    def head(h):
        return pl.ds(pl.multiple_of(h * 64, 64), 64)

    def forward(j, _):
        def one_head(h, _):
            scores = nn(kn[h, window(j), :], recv[QUERY, 2 + j, head(h), :]) * scale
            exps = jnp.exp(scores - jnp.max(scores, axis=0, keepdims=True))
            weights = (exps / jnp.sum(exps, axis=0, keepdims=True)).astype(BF16)
            probs[j, h] = weights
            mix[j, head(h), :] = nn(vt[h, :, window(j)], weights).astype(BF16)
            return 0

        lax.fori_loop(0, 3, one_head, 0)
        send_back(MIX, mix.at[j], j)
        return 0

    lax.fori_loop(0, 4, forward, 0)
    other_mix().start()

    def backward(j, _):
        def one_head(h, _):
            dmh = dm[head(h), pl.ds(pl.multiple_of(j * 128, 128), 128)]
            delta = jnp.sum(dmh.astype(F32) * mix[j, head(h), :].astype(F32), axis=0, keepdims=True)
            weights = probs[j, h]
            d_weights = nn(vn[h, window(j), :], dmh)
            d_scores = (weights.astype(F32) * (d_weights - delta) * scale).astype(BF16)
            dq[j, head(h), :] = nn(kt[h, :, window(j)], d_scores).astype(BF16)
            dkv[0, h, :, window(j)] += nt(recv[QUERY, 2 + j, head(h), :], d_scores)
            dkv[1, h, :, window(j)] += nt(dmh, weights)
            return 0

        lax.fori_loop(0, 3, one_head, 0)
        send_back(DQ, dq.at[j], j)
        return 0

    lax.fori_loop(0, 2, backward, 0)

    other_half().wait_recv()
    other_mix().wait_recv()
    rows = sum(
        nn(jnp.concatenate([mix[j], mix_other[j]], axis=1),
           jnp.concatenate([up_all[j, c], up_other[j]], axis=0)) for j in range(4))
    xs[...] = rows.astype(BF16).reshape(4, 48, 768)
    for d in range(1, 4):
        x_copy(d).start()
    lax.fori_loop(2, 4, backward, 0)

    for kv in (1, 0):
        for way in range(2):
            lanes = slice(0, 256) if way == 0 else slice(768, 1024)
            halo_out[kv, way] = dkv[kv, :, :, lanes].astype(BF16).reshape(192, 256)
            ghalo_copy(kv, way).start()

    def natural(t):
        return back[t].reshape(768, 128).T

    for kv in (1, 0):
        for way in range(2):
            ghalo_copy(kv, way).wait_recv()
        for j in range(4):
            way = j // 2
            got = halo_in[kv, 1 - way, :, 128 * (j % 2):128 * (j % 2) + 128].astype(F32)
            own = dkv[kv, :, :, 256 + 128 * j:384 + 128 * j].reshape(192, 128)
            dkv_out[kv, j] = (own + got).astype(BF16)
            send_back(DK + kv, dkv_out.at[kv, j], j)

    for d in range(1, 4):
        x_copy(d).wait_recv()
    part = xs[x].astype(F32)
    for d in range(3):
        part = part + xr[d].astype(F32)
    ys[...] = part.T.astype(BF16).reshape(8, 96, 48)
    for d in range(1, 8):
        y_copy(d).start()

    wait_back(MIX)
    load_stream(2).wait()
    mixture = natural(MIX)
    for i in range(4):
        lanes = slice(384 * i, 384 * i + 384)
        branch = nt(mixture, wall[OUT, 2 * i:2 * i + 2].reshape(384, 768))
        x_ref[0, :, lanes] = (first[:, lanes].astype(F32) - branch).astype(BF16)

    def add_unit(t, m, first=False):
        wait_back(t)
        grads = natural(t)
        for i in range(4):
            lanes = slice(384 * i, 384 * i + 384)
            term = nt(grads, wall[m, 2 * i:2 * i + 2].reshape(384, 768))
            if first:
                d_unit[:, lanes] = term
            else:
                d_unit[:, lanes] += term

    add_unit(DQ, QUERY, True)
    add_unit(DV, VALUE)

    for d in range(1, 8):
        y_copy(d).wait_recv()
    part = ys[y].astype(F32)
    for d in range(7):
        part = part + yr[d].astype(F32)
    fs[...] = part.reshape(2, 48, 48)
    far_piece().start()

    @pl.when(x != zl)
    def _():
        here_copy().start()

    @pl.when(x == zl)
    def _():
        fr[0] = fs[zh]

    add_unit(DK, KEY)
    values = second[...].astype(F32)
    center = values - jnp.mean(values, axis=-1, keepdims=True)
    inv_std = lax.rsqrt(jnp.mean(center * center, axis=-1, keepdims=True) + EPSILON)
    unit = center * inv_std
    grads = d_unit[...]
    correction = (grads - jnp.mean(grads, axis=-1, keepdims=True)
                  - unit * jnp.mean(grads * unit, axis=-1, keepdims=True))
    load_stream(3).wait()
    dx_ref[0] = (dsecond[...].astype(F32) + inv_std * correction).astype(BF16)

    far_piece().wait_recv()

    @pl.when(x != zl)
    def _():
        here_copy().wait_recv()

    grad_ref[...] = (fr[0] + fr[1]).T / 32

    def drain(m, _):
        @pl.when(edge & (c == parity))
        def _():
            far_copy(m).wait_send()

        @pl.when(edge & (c == 1))
        def _():
            near_copy(m).wait_send()

        @pl.when(c == 1)
        def _():
            cross_far(m).wait_send()
            for kind in range(2):
                core_far(m, kind).wait_send()

        core_own(m, c).wait_send()
        for s in range(4):
            for way in ways_of(s):
                if s < 3:
                    ring_copy(m, way, s).wait_send()
                else:
                    ring_last(m).wait_send()
                cross_copy(m, way, s).wait_send()
                for kind in range(2):
                    core_copy(m, kind, way, s).wait_send()
        for d in range(1, 4):
            @pl.when(m < OUT)
            def _():
                spread_copy(m, d).wait_send()

            g = (zl + d) % 4
            back_copy(m, mix.at[g], g).wait_send()
        return 0

    lax.fori_loop(0, 4, drain, 0)
    for kv in range(2):
        for way in range(2):
            halo_copy(kv, way).wait_send()
            ghalo_copy(kv, way).wait_send()
    other_half().wait_send()
    other_mix().wait_send()
    for d in range(1, 4):
        x_copy(d).wait_send()
    for d in range(1, 8):
        y_copy(d).wait_send()
    far_piece().wait_send()

    @pl.when(x != zl)
    def _():
        here_copy().wait_send()

    for way in range(2):
        for k in range(3):
            @pl.when(line_sends(way, k))
            def _():
                for part in range(2):
                    line_copy(way, k, part).wait_send()


def block(y_first, y_second, upstream, dy_second, in_proj, out_t):
    vmem = pl.BlockSpec(memory_space=pltpu.VMEM)
    dma = pltpu.SemaphoreType.DMA
    stream = jax.ShapeDtypeStruct((1, 128, 1536), BF16)
    return pl.pallas_call(
        kernel,
        out_shape=(stream, stream, jax.ShapeDtypeStruct((48, 48), F32)),
        in_specs=[pl.BlockSpec(memory_space=pl.ANY)] * 6,
        out_specs=(vmem,) * 3,
        scratch_shapes=[
            pltpu.VMEM((128, 1536), BF16),
            pltpu.VMEM((128, 1536), BF16),
            pltpu.VMEM((128, 1536), BF16),
            pltpu.VMEM((128, 1536), BF16),
            pltpu.VMEM((4, 8, 2, 2, 48, 768), BF16),
            pltpu.VMEM((8, 128, 192), BF16),
            pltpu.VMEM((3, 128, 768), F32),
            pltpu.VMEM((3, 4, 192, 128), BF16),
            pltpu.VMEM((3, 8, 192, 128), BF16),
            pltpu.VMEM((3, 1024, 64), BF16),
            pltpu.VMEM((3, 1024, 64), BF16),
            pltpu.VMEM((3, 64, 1024), BF16),
            pltpu.VMEM((3, 64, 1024), BF16),
            pltpu.VMEM((4, 3, 640, 128), BF16),
            pltpu.VMEM((4, 192, 128), BF16),
            pltpu.VMEM((4, 192, 128), BF16),
            pltpu.VMEM((2, 3, 64, 1024), F32),
            pltpu.VMEM((2, 2, 192, 256), BF16),
            pltpu.VMEM((2, 2, 192, 256), BF16),
            pltpu.VMEM((2, 4, 192, 128), BF16),
            pltpu.VMEM((4, 4, 192, 128), BF16),
            pltpu.VMEM((128, 1536), F32),
            pltpu.VMEM((4, 2, 128, 768), BF16),
            pltpu.VMEM((4, 128, 768), BF16),
            pltpu.VMEM((4, 192, 128), BF16),
            pltpu.VMEM((768, 512), BF16),
            pltpu.VMEM((192, 512), BF16),
            pltpu.VMEM((4, 48, 768), BF16),
            pltpu.VMEM((3, 48, 768), BF16),
            pltpu.VMEM((8, 96, 48), BF16),
            pltpu.VMEM((7, 96, 48), BF16),
            pltpu.VMEM((2, 48, 48), F32),
            pltpu.VMEM((2, 48, 48), F32),
            dma((4,)), dma((4,)),
            dma((4,)), dma((4,)), dma((4,)),
            dma((4, 7)), dma((4, 7)),
            dma((4, 8)), dma((4, 8)),
            dma((4, 2, 9)), dma((4, 2, 9)),
            dma((2, 3, 2)), dma((2, 3, 2)),
            dma((2,)), dma((2,)),
            dma((3, 3)), dma((3, 3)),
            dma((2, 2)), dma((2, 2)),
            dma((2, 2)), dma((2, 2)),
            dma((4, 4)), dma((4, 4)),
            dma((3,)), dma((3,)),
            dma((7,)), dma((7,)),
            dma((2,)), dma((2,)),
        ],
        compiler_params=pltpu.CompilerParams(
            collective_id=0, has_side_effects=True, vmem_limit_bytes=62 * 2**20),
        name="attention_block_backward",
    )(y_first, y_second, upstream, dy_second, in_proj, out_t)


def body(y_first, y_second, first_output_cotangent, dy_second, in_proj, out_proj):
    return block(y_first, y_second, first_output_cotangent, dy_second, in_proj, out_proj.T)


def solution(mesh):
    placed = (
        P("wide", "blk", None),
        P("wide", "blk", None),
        P("wide", "blk", None),
        P("wide", "blk", None),
        P(None, "wide", None),
        P(None, "wide"),
    )
    return jax.shard_map(
        body,
        mesh=mesh,
        in_specs=placed,
        out_specs=(P("wide", "blk", None), P("wide", "blk", None), P("blk", "wide")),
        check_vma=False,
    )
```

```python
import functools

import jax
import jax.numpy as jnp
from jax import lax
from jax.experimental import pallas as pl
from jax.experimental.pallas import tpu as pltpu
from jax.sharding import PartitionSpec as P

HDIM = 64
EPSILON = 1e-05
MESH = pl.DeviceIdType.MESH
F32 = jnp.float32
BF16 = jnp.bfloat16

KEY, VALUE, QUERY, OUT = range(4)
MIX, DQ, DK, DV = range(4)


def nt(a, b):
    return lax.dot_general(a, b, (((1,), (1,)), ((), ())), preferred_element_type=F32)


def nn(a, b):
    return jnp.dot(a, b, preferred_element_type=F32)


def kernel(first_ref, second_ref, upstream_ref, dsecond_ref, in_ref, out_ref,
           x_ref, dx_ref, grad_ref,
           first, second, upstream_in, dsecond, wall, lhs, acc, proj, recv, kn, vn, kt, vt, probs, mix, dq, dkv, halo_out,
           halo_in, dkv_out, back, d_unit, up_all, up_other, mix_other, dm_all, dm, xs, xr, ys, yr,
           fs, fr,
           load_sem, stream_sem, far_send, near_send, far_recv, ring_send, ring_recv,
           cross_send, cross_recv, core_send, core_recv,
           line_send, line_recv, swap_send, swap_recv, spread_send, spread_recv, halo_send, halo_recv,
           ghalo_send, ghalo_recv, back_send, back_recv,
           xs_send, xs_recv, ys_send, ys_recv, fs_send, fs_recv):
    b, w = lax.axis_index("blk"), lax.axis_index("wide")
    x, zl, y, zh, c = b // 4, b % 4, w // 4, (w // 2) % 2, w % 2
    edge = (zl == 0) | (zl == 3)
    half = (zh, 1 - zh)
    carried, parity = (zh + c) % 2, x % 2

    def at_x(d):
        return {"blk": ((x + d) % 4) * 4 + zl}

    def at_y(d):
        return {"wide": ((y + d) % 8) * 4 + zh * 2 + c}

    def at_z(d):
        return {"blk": x * 4 + (zl + d) % 4}

    above, below = at_y(1), at_y(7)
    partner = {"wide": w + 1 - 2 * c}
    crosses = edge & ((parity == 0) | (c == 1))
    far = {"blk": b + 3 - 2 * zl,
           "wide": y * 4 + (1 - zh) * 2 + jnp.where(parity == 0, 1 - c, c)}
    near = {"blk": b + 1 - 2 * (b % 2)}

    def copy(src, dst, send, got, device):
        return pltpu.make_async_remote_copy(
            src_ref=src, dst_ref=dst, send_sem=send, recv_sem=got,
            device_id=device, device_id_type=MESH)

    barrier = pltpu.get_barrier_semaphore()
    greeted = [partner] + [at_x(d) for d in range(1, 4)] + [at_y(d) for d in range(1, 8)]
    greeted += [at_z(d) for d in range(1, 4)]
    turned_here = {"blk": zl * 4 + x}
    turned_far = {"blk": zl * 4 + x, "wide": w + 2 - 4 * zh}
    for device in greeted:
        pl.semaphore_signal(barrier, inc=1, device_id=device, device_id_type=MESH)

    @pl.when(crosses)
    def _():
        pl.semaphore_signal(barrier, inc=1, device_id=far, device_id_type=MESH)

    pl.semaphore_signal(barrier, inc=1, device_id=turned_far, device_id_type=MESH)

    @pl.when(x != zl)
    def _():
        pl.semaphore_signal(barrier, inc=1, device_id=turned_here, device_id_type=MESH)

    def load_weight(m):
        source = (in_ref.at[1], in_ref.at[2], in_ref.at[0], out_ref)[m]
        return pltpu.make_async_copy(source, wall.at[m, y, zh, c], load_sem.at[m])

    streams = ((second_ref, second), (upstream_ref, upstream_in), (first_ref, first),
               (dsecond_ref, dsecond))

    def load_stream(i):
        return pltpu.make_async_copy(streams[i][0].at[0], streams[i][1], stream_sem.at[i])

    for m in range(4):
        load_weight(m).start()
    for i in range(4):
        load_stream(i).start()
    for m in range(4):
        load_weight(m).wait()
    extra = 1 + crosses.astype(jnp.int32) + (x != zl).astype(jnp.int32)
    pl.semaphore_wait(barrier, len(greeted) + extra)

    def far_copy(m):
        block = wall.at[m, y, zh, c]
        return copy(block, block, far_send.at[m], far_recv.at[m], far)

    def near_copy(m):
        block = wall.at[m, y, 1 - zh, parity]
        return copy(block, block, near_send.at[m], far_recv.at[m], near)

    def place(way, s):
        return (y + 7 - s) % 8 if way == 0 else (y + 1 + s) % 8

    def slot(way, s):
        return s if way == 0 else 4 + s

    def ring_copy(m, way, s):
        origin = (y + 8 - s) % 8 if way == 0 else (y + s) % 8
        block = wall.at[m, origin, carried, parity]
        j = slot(way, s)
        return copy(block, block, ring_send.at[m, j], ring_recv.at[m, j],
                    above if way == 0 else below)

    def ring_got(m, way, s):
        block = wall.at[m, place(way, s), carried, parity]
        j = slot(way, s)
        return copy(block, block, ring_send.at[m, j], ring_recv.at[m, j], above)

    def ring_last(m):
        block = wall.at[m, (y + 5 + 6 * c) % 8, carried, parity]
        return copy(block, block, ring_send.at[m, 3], ring_recv.at[m, 3],
                    {"wide": ((y + 1 + 6 * c) % 8) * 4 + zh * 2 + c})

    def cross_copy(m, way, s):
        block = wall.at[m, place(way, s), carried, parity]
        j = slot(way, s)
        to = 1 + 2 * c if s == 3 else (1, 3)[way]
        return copy(block, block, cross_send.at[m, j], cross_recv.at[m, j], at_x(to))

    def cross_got(m, way, s):
        block = wall.at[m, place(way, s), carried, 1 - parity]
        j = slot(way, s)
        return copy(block, block, cross_send.at[m, j], cross_recv.at[m, j], at_x(1))

    def core_copy(m, kind, way, s, mine=True):
        half_of = carried if mine else 1 - carried
        block = wall.at[m, place(way, s), half_of, 1 - parity if kind else parity]
        j = slot(way, s)
        return copy(block, block, core_send.at[m, kind, j], core_recv.at[m, kind, j], partner)

    def core_own(m, core):
        block = wall.at[m, y, zh, core]
        return copy(block, block, core_send.at[m, 0, 7], core_recv.at[m, 0, 7], partner)

    def core_far(m, kind):
        block = wall.at[m, y, 1 - zh, 1 - parity if kind else parity]
        return copy(block, block, core_send.at[m, 1, 7 + kind], core_recv.at[m, 1, 7 + kind],
                    partner)

    def cross_far(m, own=True):
        block = wall.at[m, y, 1 - zh, parity if own else 1 - parity]
        return copy(block, block, cross_send.at[m, 7], cross_recv.at[m, 7], at_x(1))

    def ways_of(s):
        return (0, 1) if s < 3 else (0,)

    def start_stream(m):
        for way in range(2):
            ring_copy(m, way, 0).start()

    def have_own(m):
        core_own(m, 1 - c).wait_recv()

        @pl.when(c == 0)
        def _():
            start_stream(m)

    def begin_far(m):
        start_stream(m)
        core_far(m, 0).start()
        cross_far(m).start()

    def inner_far(m):
        @pl.when((c == 1) & jnp.logical_not(edge))
        def _():
            near_copy(m).wait_recv()

    def have_far(m):
        @pl.when(c == 1)
        def _():
            cross_far(m, False).wait_recv()
            core_far(m, 1).start()

        @pl.when(c == 0)
        def _():
            core_far(m, 0).wait_recv()
            core_far(m, 1).wait_recv()

    def ring_step(m, s):
        for way in ways_of(s):
            ring_got(m, way, s).wait_recv()
            if s < 2:
                ring_copy(m, way, s + 1).start()
            if s == 2:
                @pl.when(c == way)
                def _():
                    ring_last(m).start()
            cross_copy(m, way, s).start()
            core_copy(m, 0, way, s).start()

    def cross_step(m, s):
        for way in ways_of(s):
            cross_got(m, way, s).wait_recv()
            core_copy(m, 1, way, s).start()

    def project(m, origin, first=False):
        term = nn(lhs[origin], wall[m, origin].reshape(192, 768))
        if first:
            acc[m] = term
        else:
            acc[m] += term

    def project_step(m, s):
        for way in ways_of(s):
            for kind in range(2):
                core_copy(m, kind, way, s, False).wait_recv()

            @pl.when(m < OUT)
            def _():
                project(m, place(way, s))

    def spread_copy(m, d):
        return copy(proj.at[m, (zl + d) % 4], recv.at[m, 2 + zl], spread_send.at[m, d - 1],
                    spread_recv.at[m, d - 1], at_z(d))

    def spread_arrived(m, d):
        return copy(proj.at[m, (zl + d) % 4], recv.at[m, 2 + (zl + 4 - d) % 4],
                    spread_send.at[m, d - 1], spread_recv.at[m, d - 1], at_z(d))

    def halo_copy(m, way, arriving=False):
        start = (4, 2)[way]
        into = (0, 6)[way]
        return copy(recv.at[m, start:start + 2], recv.at[m, into:into + 2],
                    halo_send.at[m, way], halo_recv.at[m, way], at_x((1, 3)[way]))

    def ghalo_copy(kv, way):
        return copy(halo_out.at[kv, way], halo_in.at[kv, way], ghalo_send.at[kv, way],
                    ghalo_recv.at[kv, way], at_x((3, 1)[way]))

    def back_copy(t, source, j):
        return copy(source, back.at[t, zl], back_send.at[t, j], back_recv.at[t, zl],
                    {"blk": x * 4 + j})

    def send_back(t, source, j):
        @pl.when(j != zl)
        def _():
            back_copy(t, source, j).start()

        @pl.when(j == zl)
        def _():
            back[t, zl] = source[...]

    def wait_back(t):
        for d in range(1, 4):
            g = (zl + d) % 4
            copy(back.at[t, g], back.at[t, g], back_send.at[t, g], back_recv.at[t, g],
                 {"blk": x * 4 + g}).wait_recv()

    def line_sends(way, k):
        return (zl < 3) & (zl >= k) if way == 0 else (zl > 0) & (zl + k <= 3)

    def line_gets(way, k):
        return zl >= k + 1 if way == 0 else zl + k <= 2

    def line_copy(way, k, part):
        block = up_all.at[zl - k if way == 0 else zl + k, part]
        return copy(block, block, line_send.at[way, k, part], line_recv.at[way, k, part],
                    {"blk": b + 1 if way == 0 else b - 1})

    def line_got(way, k, part):
        block = up_all.at[zl - 1 - k if way == 0 else zl + 1 + k, part]
        return copy(block, block, line_send.at[way, k, part], line_recv.at[way, k, part],
                    {"blk": b + 1 if way == 0 else b - 1})

    def line_step(k, part):
        for way in range(2):
            @pl.when(line_gets(way, k))
            def _():
                line_got(way, k, part).wait_recv()

                @pl.when(line_sends(way, k + 1))
                def _():
                    line_copy(way, k + 1, part).start()

    def other_half():
        return copy(up_all.at[:, 1 - c], up_other, swap_send.at[0], swap_recv.at[0], partner)

    def other_mix(j):
        return copy(mix.at[j], mix_other.at[j], swap_send.at[1 + j], swap_recv.at[1 + j], partner)

    def x_copy(d):
        return copy(xs.at[(x + d) % 4], xr.at[d - 1], xs_send.at[d - 1], xs_recv.at[d - 1], at_x(d))

    def y_copy(d):
        return copy(ys.at[(y + d) % 8], yr.at[d - 1], ys_send.at[d - 1], ys_recv.at[d - 1], at_y(d))

    def here_copy():
        return copy(fs.at[zh], fr.at[0], fs_send.at[0], fs_recv.at[0], turned_here)

    def far_piece():
        return copy(fs.at[1 - zh], fr.at[1], fs_send.at[1], fs_recv.at[1], turned_far)

    @pl.when(edge & (c == parity))
    def _():
        for m in range(4):
            far_copy(m).start()

    for m in range(4):
        core_own(m, c).start()
    have_own(0)

    @pl.when(edge & (c == 1))
    def _():
        for m in range(4):
            near_copy(m).wait_recv()
            near_copy(m).start()
            if m == 0:
                begin_far(0)

    load_stream(1).wait()
    by_core = upstream_in[...].T.reshape(16, 2, 48, 128)
    for core in range(2):
        up_all[zl, core] = by_core[:, core].reshape(768, 128).T
    for part in range(2):
        for way in range(2):
            @pl.when(line_sends(way, 0))
            def _():
                line_copy(way, 0, part).start()

    load_stream(0).wait()
    values = second[...].astype(F32)
    center = values - jnp.mean(values, axis=-1, keepdims=True)
    inv_std = lax.rsqrt(jnp.mean(center * center, axis=-1, keepdims=True) + EPSILON)
    unit_b = (center * inv_std).astype(BF16)
    for i in range(8):
        lhs[i] = unit_b[:, 192 * i:192 * i + 192]

    @pl.when((c == 1) & jnp.logical_not(edge))
    def _():
        near_copy(0).wait_recv()
        begin_far(0)

    def finish(m):
        proj[m] = acc[m].T.astype(BF16).reshape(4, 192, 128)
        for d in range(1, 4):
            spread_copy(m, d).start()
        recv[m, 2 + zl] = proj[m, zl]

    def gather_step(t, _):
        def at(late, f, s, last=OUT):
            m = t - late - s

            @pl.when((m >= 0) & (m <= last))
            def _():
                f(m, s)

        for s in (3, 2, 1, 0):
            at(0, ring_step, s)

        @pl.when(t < 3)
        def _():
            have_own(t + 1)
            inner_far(t + 1)

            @pl.when(c == 1)
            def _():
                begin_far(t + 1)

        @pl.when(t < 6)
        def _():
            line_step(t // 2, t % 2)

        at(1, lambda m, s: have_far(m), 0)
        at(1, lambda m, s: project(m, y, True), 0, QUERY)
        for s in (3, 2, 1, 0):
            at(2, project_step, s)
        at(5, lambda m, s: finish(m), 0, QUERY)
        for s in (3, 2, 1, 0):
            at(1, cross_step, s)

        @pl.when(t == 6)
        def _():
            other_half().start()

        @pl.when(t >= 7)
        def _():
            m = t - 7
            for d in range(1, 4):
                spread_arrived(m, d).wait_recv()
            for way in range(2):
                halo_copy(m, way).start()

        return 0

    lax.fori_loop(0, 9, gather_step, 0)

    for j in range(4):
        dm_all[:, 128 * j:128 * j + 128] = sum(
            nn(up_all[j, core], wall[OUT, :, :, core].reshape(768, 768)) for core in range(2)
        ).T.astype(BF16)
    dm[...] = dm_all[pl.ds(pl.multiple_of(zl * 192, 64), 192), :]

    for m in (KEY, VALUE):
        for way in range(2):
            halo_copy(m, way).wait_recv()
    for e in range(8):
        for m, natural, turned in ((KEY, kn, kt), (VALUE, vn, vt)):
            block = recv[m, e]
            flat = block.T
            for h in range(3):
                turned[h, :, 128 * e:128 * e + 128] = block[64 * h:64 * h + 64]
                natural[h, 128 * e:128 * e + 128, :] = flat[:, 64 * h:64 * h + 64]

    for d in range(1, 4):
        spread_arrived(QUERY, d).wait_recv()
    scale = HDIM ** -0.5
    dkv[...] = jnp.zeros_like(dkv)

    def window(j):
        return pl.ds(pl.multiple_of(j * 128, 128), 640)

    def of_block(j):
        return pl.ds(pl.multiple_of(j * 128, 128), 128)

    def forward(j, _):
        for h in range(3):
            rows = slice(64 * h, 64 * h + 64)
            scores = nn(kn[h, window(j), :], recv[QUERY, 2 + j, rows, :] * scale)
            exps = jnp.exp(scores - jnp.max(scores, axis=0, keepdims=True))
            weights = (exps * (1 / jnp.sum(exps, axis=0, keepdims=True))).astype(BF16)
            probs[j, h] = weights
            mix[j, rows, :] = nn(vt[h, :, window(j)], weights).astype(BF16)
            dkv[1, h, :, window(j)] += nt(dm[rows, of_block(j)], weights)
        other_mix(j).start()
        send_back(MIX, mix.at[j], j)
        return 0

    def backward(j, _):
        for h in range(3):
            rows = slice(64 * h, 64 * h + 64)
            dmh = dm[rows, of_block(j)] * scale
            delta = jnp.sum(dmh.astype(F32) * mix[j, rows, :].astype(F32), axis=0, keepdims=True)
            d_weights = nn(vn[h, window(j), :], dmh)
            d_scores = (probs[j, h].astype(F32) * (d_weights - delta)).astype(BF16)
            dq[j, rows, :] = nn(kt[h, :, window(j)], d_scores).astype(BF16)
            dkv[0, h, :, window(j)] += nt(recv[QUERY, 2 + j, rows, :], d_scores)
        send_back(DQ, dq.at[j], j)
        return 0

    def send_halo(kv, way):
        lanes = slice(0, 256) if way == 0 else slice(768, 1024)
        halo_out[kv, way] = dkv[kv, :, :, lanes].astype(BF16).reshape(192, 256)
        ghalo_copy(kv, way).start()

    def finish_halo(kv):
        for way in range(2):
            ghalo_copy(kv, way).wait_recv()
            for i in range(2):
                j = i + 2 - 2 * way
                got = halo_in[kv, way, :, 128 * i:128 * i + 128].astype(F32)
                own = dkv[kv, :, :, 256 + 128 * j:384 + 128 * j].reshape(192, 128)
                dkv_out[kv, j] = (own + got).astype(BF16)
                send_back(DK + kv, dkv_out.at[kv, j], j)

    lax.fori_loop(0, 2, forward, 0)
    send_halo(1, 0)
    lax.fori_loop(2, 4, forward, 0)
    send_halo(1, 1)
    lax.fori_loop(0, 2, backward, 0)
    send_halo(0, 0)

    other_half().wait_recv()
    for j in range(4):
        other_mix(j).wait_recv()
    rows = sum(
        nn(jnp.concatenate([mix[j], mix_other[j]], axis=1),
           jnp.concatenate([up_all[j, c], up_other[j]], axis=0)) for j in range(4))
    xs[...] = rows.astype(BF16).reshape(4, 48, 768)
    for d in range(1, 4):
        x_copy(d).start()

    lax.fori_loop(2, 4, backward, 0)
    send_halo(0, 1)
    finish_halo(1)

    def drain(m, _):
        @pl.when(edge & (c == parity))
        def _():
            far_copy(m).wait_send()

        @pl.when(edge & (c == 1))
        def _():
            near_copy(m).wait_send()

        @pl.when(c == 1)
        def _():
            cross_far(m).wait_send()
            for kind in range(2):
                core_far(m, kind).wait_send()

        core_own(m, c).wait_send()
        for s in range(4):
            for way in ways_of(s):
                if s < 3:
                    ring_copy(m, way, s).wait_send()
                else:
                    ring_last(m).wait_send()
                cross_copy(m, way, s).wait_send()
                for kind in range(2):
                    core_copy(m, kind, way, s).wait_send()
        for d in range(1, 4):
            @pl.when(m < OUT)
            def _():
                spread_copy(m, d).wait_send()

        return 0

    def natural(t):
        return back[t].reshape(768, 128).T

    lax.fori_loop(0, 4, drain, 0)

    for d in range(1, 4):
        x_copy(d).wait_recv()
    part = xs[x].astype(F32)
    for d in range(3):
        part = part + xr[d].astype(F32)
    for i in range(8):
        ys[i] = part[:, 96 * i:96 * i + 96].astype(BF16)
    for d in range(1, 8):
        y_copy(d).start()

    finish_halo(0)

    wait_back(MIX)
    load_stream(2).wait()
    mixture = natural(MIX)
    for i in range(4):
        lanes = slice(384 * i, 384 * i + 384)
        branch = nt(mixture, wall[OUT, 2 * i:2 * i + 2].reshape(384, 768))
        x_ref[0, :, lanes] = (first[:, lanes].astype(F32) - branch).astype(BF16)

    def add_unit(t, m, first=False):
        wait_back(t)
        grads = natural(t)
        for i in range(4):
            lanes = slice(384 * i, 384 * i + 384)
            term = nt(grads, wall[m, 2 * i:2 * i + 2].reshape(384, 768))
            if first:
                d_unit[:, lanes] = term
            else:
                d_unit[:, lanes] += term

    add_unit(DQ, QUERY, True)
    add_unit(DV, VALUE)

    for d in range(1, 8):
        y_copy(d).wait_recv()
    part = ys[y].astype(F32)
    for d in range(7):
        part = part + yr[d].astype(F32)
    for i in range(2):
        fs[i] = part[:, 48 * i:48 * i + 48]
    far_piece().start()

    @pl.when(x != zl)
    def _():
        here_copy().start()

    @pl.when(x == zl)
    def _():
        fr[0] = fs[zh]

    add_unit(DK, KEY)
    values = second[...].astype(F32)
    center = values - jnp.mean(values, axis=-1, keepdims=True)
    inv_std = lax.rsqrt(jnp.mean(center * center, axis=-1, keepdims=True) + EPSILON)
    unit = center * inv_std
    grads = d_unit[...]
    correction = (grads - jnp.mean(grads, axis=-1, keepdims=True)
                  - unit * jnp.mean(grads * unit, axis=-1, keepdims=True))
    load_stream(3).wait()
    dx_ref[0] = (dsecond[...].astype(F32) + inv_std * correction).astype(BF16)

    far_piece().wait_recv()

    @pl.when(x != zl)
    def _():
        here_copy().wait_recv()

    grad_ref[...] = (fr[0] + fr[1]) / 32

    for kv in range(2):
        for way in range(2):
            halo_copy(kv, way).wait_send()
            ghalo_copy(kv, way).wait_send()
    other_half().wait_send()
    for j in range(4):
        other_mix(j).wait_send()
    for t in (MIX, DQ, DK, DV):
        for d in range(1, 4):
            g = (zl + d) % 4
            back_copy(t, mix.at[g], g).wait_send()
    for d in range(1, 4):
        x_copy(d).wait_send()
    for d in range(1, 8):
        y_copy(d).wait_send()
    far_piece().wait_send()

    @pl.when(x != zl)
    def _():
        here_copy().wait_send()

    for way in range(2):
        for k in range(3):
            @pl.when(line_sends(way, k))
            def _():
                for part in range(2):
                    line_copy(way, k, part).wait_send()


def block(y_first, y_second, upstream, dy_second, in_proj, out_t):
    vmem = pl.BlockSpec(memory_space=pltpu.VMEM)
    dma = pltpu.SemaphoreType.DMA
    stream = jax.ShapeDtypeStruct((1, 128, 1536), BF16)
    return pl.pallas_call(
        kernel,
        out_shape=(stream, stream, jax.ShapeDtypeStruct((48, 48), F32)),
        in_specs=[pl.BlockSpec(memory_space=pl.ANY)] * 6,
        out_specs=(vmem,) * 3,
        scratch_shapes=[
            pltpu.VMEM((128, 1536), BF16),
            pltpu.VMEM((128, 1536), BF16),
            pltpu.VMEM((128, 1536), BF16),
            pltpu.VMEM((128, 1536), BF16),
            pltpu.VMEM((4, 8, 2, 2, 48, 768), BF16),
            pltpu.VMEM((8, 128, 192), BF16),
            pltpu.VMEM((3, 128, 768), F32),
            pltpu.VMEM((3, 4, 192, 128), BF16),
            pltpu.VMEM((3, 8, 192, 128), BF16),
            pltpu.VMEM((3, 1024, 64), BF16),
            pltpu.VMEM((3, 1024, 64), BF16),
            pltpu.VMEM((3, 64, 1024), BF16),
            pltpu.VMEM((3, 64, 1024), BF16),
            pltpu.VMEM((4, 3, 640, 128), BF16),
            pltpu.VMEM((4, 192, 128), BF16),
            pltpu.VMEM((4, 192, 128), BF16),
            pltpu.VMEM((2, 3, 64, 1024), F32),
            pltpu.VMEM((2, 2, 192, 256), BF16),
            pltpu.VMEM((2, 2, 192, 256), BF16),
            pltpu.VMEM((2, 4, 192, 128), BF16),
            pltpu.VMEM((4, 4, 192, 128), BF16),
            pltpu.VMEM((128, 1536), F32),
            pltpu.VMEM((4, 2, 128, 768), BF16),
            pltpu.VMEM((4, 128, 768), BF16),
            pltpu.VMEM((4, 192, 128), BF16),
            pltpu.VMEM((768, 512), BF16),
            pltpu.VMEM((192, 512), BF16),
            pltpu.VMEM((4, 48, 768), BF16),
            pltpu.VMEM((3, 48, 768), BF16),
            pltpu.VMEM((8, 48, 96), BF16),
            pltpu.VMEM((7, 48, 96), BF16),
            pltpu.VMEM((2, 48, 48), F32),
            pltpu.VMEM((2, 48, 48), F32),
            dma((4,)), dma((4,)),
            dma((4,)), dma((4,)), dma((4,)),
            dma((4, 7)), dma((4, 7)),
            dma((4, 8)), dma((4, 8)),
            dma((4, 2, 9)), dma((4, 2, 9)),
            dma((2, 3, 2)), dma((2, 3, 2)),
            dma((5,)), dma((5,)),
            dma((3, 3)), dma((3, 3)),
            dma((2, 2)), dma((2, 2)),
            dma((2, 2)), dma((2, 2)),
            dma((4, 4)), dma((4, 4)),
            dma((3,)), dma((3,)),
            dma((7,)), dma((7,)),
            dma((2,)), dma((2,)),
        ],
        compiler_params=pltpu.CompilerParams(
            collective_id=0, has_side_effects=True, vmem_limit_bytes=62 * 2**20),
        name="attention_block_backward",
    )(y_first, y_second, upstream, dy_second, in_proj, out_t)


def body(y_first, y_second, first_output_cotangent, dy_second, in_proj, out_proj):
    return block(y_first, y_second, first_output_cotangent, dy_second, in_proj, out_proj.T)


def solution(mesh):
    placed = (
        P("wide", "blk", None),
        P("wide", "blk", None),
        P("wide", "blk", None),
        P("wide", "blk", None),
        P(None, "wide", None),
        P(None, "wide"),
    )
    return jax.shard_map(
        body,
        mesh=mesh,
        in_specs=placed,
        out_specs=(P("wide", "blk", None), P("wide", "blk", None), P("blk", "wide")),
        check_vma=False,
    )
```

```python
import functools

import jax
import jax.numpy as jnp
from jax import lax
from jax.experimental import pallas as pl
from jax.experimental.pallas import tpu as pltpu
from jax.sharding import PartitionSpec as P

HDIM = 64
EPSILON = 1e-05
MESH = pl.DeviceIdType.MESH
F32 = jnp.float32
BF16 = jnp.bfloat16

KEY, VALUE, QUERY, OUT = range(4)
MIX, DQ, DK, DV = range(4)


def nt(a, b):
    return lax.dot_general(a, b, (((1,), (1,)), ((), ())), preferred_element_type=F32)


def nn(a, b):
    return jnp.dot(a, b, preferred_element_type=F32)


def kernel(first_ref, second_ref, upstream_ref, dsecond_ref, in_ref, out_ref,
           x_ref, dx_ref, grad_ref,
           first, second, upstream_in, dsecond, unit, spread_std, wall, lhs, acc, proj, recv, kn, vn, kt, vt, probs, mix, dq, dkv, halo_out,
           halo_in, dkv_out, back, d_unit, up_all, up_other, mix_other, dm_all, dm, xs, xr, ys, yr,
           fs, fr,
           load_sem, stream_sem, far_send, near_send, far_recv, ring_send, ring_recv,
           cross_send, cross_recv, core_send, core_recv,
           line_send, line_recv, swap_send, swap_recv, spread_send, spread_recv, halo_send, halo_recv,
           ghalo_send, ghalo_recv, back_send, back_recv,
           xs_send, xs_recv, ys_send, ys_recv, fs_send, fs_recv):
    b, w = lax.axis_index("blk"), lax.axis_index("wide")
    x, zl, y, zh, c = b // 4, b % 4, w // 4, (w // 2) % 2, w % 2
    edge = (zl == 0) | (zl == 3)
    half = (zh, 1 - zh)
    carried, parity = (zh + c) % 2, x % 2

    def at_x(d):
        return {"blk": ((x + d) % 4) * 4 + zl}

    def at_y(d):
        return {"wide": ((y + d) % 8) * 4 + zh * 2 + c}

    def at_z(d):
        return {"blk": x * 4 + (zl + d) % 4}

    above, below = at_y(1), at_y(7)
    partner = {"wide": w + 1 - 2 * c}
    crosses = edge & ((parity == 0) | (c == 1))
    far = {"blk": b + 3 - 2 * zl,
           "wide": y * 4 + (1 - zh) * 2 + jnp.where(parity == 0, 1 - c, c)}
    near = {"blk": b + 1 - 2 * (b % 2)}

    def copy(src, dst, send, got, device):
        return pltpu.make_async_remote_copy(
            src_ref=src, dst_ref=dst, send_sem=send, recv_sem=got,
            device_id=device, device_id_type=MESH)

    barrier = pltpu.get_barrier_semaphore()
    greeted = [partner] + [at_x(d) for d in range(1, 4)] + [at_y(d) for d in range(1, 8)]
    greeted += [at_z(d) for d in range(1, 4)]
    turned_here = {"blk": zl * 4 + x}
    turned_far = {"blk": zl * 4 + x, "wide": w + 2 - 4 * zh}
    for device in greeted:
        pl.semaphore_signal(barrier, inc=1, device_id=device, device_id_type=MESH)

    @pl.when(crosses)
    def _():
        pl.semaphore_signal(barrier, inc=1, device_id=far, device_id_type=MESH)

    pl.semaphore_signal(barrier, inc=1, device_id=turned_far, device_id_type=MESH)

    @pl.when(x != zl)
    def _():
        pl.semaphore_signal(barrier, inc=1, device_id=turned_here, device_id_type=MESH)

    def load_weight(m):
        source = (in_ref.at[1], in_ref.at[2], in_ref.at[0], out_ref)[m]
        return pltpu.make_async_copy(source, wall.at[m, y, zh, c], load_sem.at[m])

    streams = ((second_ref, second), (upstream_ref, upstream_in), (first_ref, first),
               (dsecond_ref, dsecond))

    def load_stream(i):
        return pltpu.make_async_copy(streams[i][0].at[0], streams[i][1], stream_sem.at[i])

    for m in range(4):
        load_weight(m).start()
    for i in range(4):
        load_stream(i).start()
    for m in range(4):
        load_weight(m).wait()
    extra = 1 + crosses.astype(jnp.int32) + (x != zl).astype(jnp.int32)
    pl.semaphore_wait(barrier, len(greeted) + extra)

    def far_copy(m):
        block = wall.at[m, y, zh, c]
        return copy(block, block, far_send.at[m], far_recv.at[m], far)

    def near_copy(m):
        block = wall.at[m, y, 1 - zh, parity]
        return copy(block, block, near_send.at[m], far_recv.at[m], near)

    def place(way, s):
        return (y + 7 - s) % 8 if way == 0 else (y + 1 + s) % 8

    def slot(way, s):
        return s if way == 0 else 4 + s

    def ring_copy(m, way, s):
        origin = (y + 8 - s) % 8 if way == 0 else (y + s) % 8
        block = wall.at[m, origin, carried, parity]
        j = slot(way, s)
        return copy(block, block, ring_send.at[m, j], ring_recv.at[m, j],
                    above if way == 0 else below)

    def ring_got(m, way, s):
        block = wall.at[m, place(way, s), carried, parity]
        j = slot(way, s)
        return copy(block, block, ring_send.at[m, j], ring_recv.at[m, j], above)

    def ring_last(m):
        block = wall.at[m, (y + 5 + 6 * c) % 8, carried, parity]
        return copy(block, block, ring_send.at[m, 3], ring_recv.at[m, 3],
                    {"wide": ((y + 1 + 6 * c) % 8) * 4 + zh * 2 + c})

    def cross_copy(m, way, s):
        block = wall.at[m, place(way, s), carried, parity]
        j = slot(way, s)
        to = 1 + 2 * c if s == 3 else (1, 3)[way]
        return copy(block, block, cross_send.at[m, j], cross_recv.at[m, j], at_x(to))

    def cross_got(m, way, s):
        block = wall.at[m, place(way, s), carried, 1 - parity]
        j = slot(way, s)
        return copy(block, block, cross_send.at[m, j], cross_recv.at[m, j], at_x(1))

    def core_copy(m, kind, way, s, mine=True):
        half_of = carried if mine else 1 - carried
        block = wall.at[m, place(way, s), half_of, 1 - parity if kind else parity]
        j = slot(way, s)
        return copy(block, block, core_send.at[m, kind, j], core_recv.at[m, kind, j], partner)

    def core_own(m, core):
        block = wall.at[m, y, zh, core]
        return copy(block, block, core_send.at[m, 0, 7], core_recv.at[m, 0, 7], partner)

    def core_far(m, kind):
        block = wall.at[m, y, 1 - zh, 1 - parity if kind else parity]
        return copy(block, block, core_send.at[m, 1, 7 + kind], core_recv.at[m, 1, 7 + kind],
                    partner)

    def cross_far(m, own=True):
        block = wall.at[m, y, 1 - zh, parity if own else 1 - parity]
        return copy(block, block, cross_send.at[m, 7], cross_recv.at[m, 7], at_x(1))

    def ways_of(s):
        return (0, 1) if s < 3 else (0,)

    def start_stream(m):
        for way in range(2):
            ring_copy(m, way, 0).start()

    def have_own(m):
        core_own(m, 1 - c).wait_recv()

        @pl.when(c == 0)
        def _():
            start_stream(m)

    def begin_far(m):
        start_stream(m)
        core_far(m, 0).start()
        cross_far(m).start()

    def inner_far(m):
        @pl.when((c == 1) & jnp.logical_not(edge))
        def _():
            near_copy(m).wait_recv()

    def have_far(m):
        @pl.when(c == 1)
        def _():
            cross_far(m, False).wait_recv()
            core_far(m, 1).start()

        @pl.when(c == 0)
        def _():
            core_far(m, 0).wait_recv()
            core_far(m, 1).wait_recv()

    def ring_step(m, s):
        for way in ways_of(s):
            ring_got(m, way, s).wait_recv()
            if s < 2:
                ring_copy(m, way, s + 1).start()
            if s == 2:
                @pl.when(c == way)
                def _():
                    ring_last(m).start()
            cross_copy(m, way, s).start()
            core_copy(m, 0, way, s).start()

    def cross_step(m, s):
        for way in ways_of(s):
            cross_got(m, way, s).wait_recv()
            core_copy(m, 1, way, s).start()

    def project(m, origin, first=False):
        term = nn(lhs[origin], wall[m, origin].reshape(192, 768))
        if first:
            acc[m] = term
        else:
            acc[m] += term

    def project_step(m, s):
        for way in ways_of(s):
            for kind in range(2):
                core_copy(m, kind, way, s, False).wait_recv()

            @pl.when(m < OUT)
            def _():
                project(m, place(way, s))

    def spread_copy(m, d):
        return copy(proj.at[m, (zl + d) % 4], recv.at[m, 2 + zl], spread_send.at[m, d - 1],
                    spread_recv.at[m, d - 1], at_z(d))

    def spread_arrived(m, d):
        return copy(proj.at[m, (zl + d) % 4], recv.at[m, 2 + (zl + 4 - d) % 4],
                    spread_send.at[m, d - 1], spread_recv.at[m, d - 1], at_z(d))

    def halo_copy(m, way, arriving=False):
        start = (4, 2)[way]
        into = (0, 6)[way]
        return copy(recv.at[m, start:start + 2], recv.at[m, into:into + 2],
                    halo_send.at[m, way], halo_recv.at[m, way], at_x((1, 3)[way]))

    def ghalo_copy(kv, way):
        return copy(halo_out.at[kv, way], halo_in.at[kv, way], ghalo_send.at[kv, way],
                    ghalo_recv.at[kv, way], at_x((3, 1)[way]))

    def back_copy(t, source, j):
        return copy(source, back.at[t, zl], back_send.at[t, j], back_recv.at[t, zl],
                    {"blk": x * 4 + j})

    def send_back(t, source, j):
        @pl.when(j != zl)
        def _():
            back_copy(t, source, j).start()

        @pl.when(j == zl)
        def _():
            back[t, zl] = source[...]

    def wait_back(t):
        for d in range(1, 4):
            g = (zl + d) % 4
            copy(back.at[t, g], back.at[t, g], back_send.at[t, g], back_recv.at[t, g],
                 {"blk": x * 4 + g}).wait_recv()

    def line_sends(way, k):
        return (zl < 3) & (zl >= k) if way == 0 else (zl > 0) & (zl + k <= 3)

    def line_gets(way, k):
        return zl >= k + 1 if way == 0 else zl + k <= 2

    def line_copy(way, k, part):
        block = up_all.at[zl - k if way == 0 else zl + k, part]
        return copy(block, block, line_send.at[way, k, part], line_recv.at[way, k, part],
                    {"blk": b + 1 if way == 0 else b - 1})

    def line_got(way, k, part):
        block = up_all.at[zl - 1 - k if way == 0 else zl + 1 + k, part]
        return copy(block, block, line_send.at[way, k, part], line_recv.at[way, k, part],
                    {"blk": b + 1 if way == 0 else b - 1})

    def line_step(k, part):
        for way in range(2):
            @pl.when(line_gets(way, k))
            def _():
                line_got(way, k, part).wait_recv()

                @pl.when(line_sends(way, k + 1))
                def _():
                    line_copy(way, k + 1, part).start()

    def other_half():
        return copy(up_all.at[:, 1 - c], up_other, swap_send.at[0], swap_recv.at[0], partner)

    def other_mix(j):
        return copy(mix.at[j], mix_other.at[j], swap_send.at[1 + j], swap_recv.at[1 + j], partner)

    def x_copy(d):
        return copy(xs.at[(x + d) % 4], xr.at[d - 1], xs_send.at[d - 1], xs_recv.at[d - 1], at_x(d))

    def y_copy(d):
        return copy(ys.at[(y + d) % 8], yr.at[d - 1], ys_send.at[d - 1], ys_recv.at[d - 1], at_y(d))

    def here_copy():
        return copy(fs.at[zh], fr.at[0], fs_send.at[0], fs_recv.at[0], turned_here)

    def far_piece():
        return copy(fs.at[1 - zh], fr.at[1], fs_send.at[1], fs_recv.at[1], turned_far)

    @pl.when(edge & (c == parity))
    def _():
        for m in range(4):
            far_copy(m).start()

    for m in range(4):
        core_own(m, c).start()
    have_own(0)

    @pl.when(edge & (c == 1))
    def _():
        for m in range(4):
            near_copy(m).wait_recv()
            near_copy(m).start()
            if m == 0:
                begin_far(0)

    load_stream(1).wait()
    by_core = upstream_in[...].T.reshape(16, 2, 48, 128)
    for core in range(2):
        up_all[zl, core] = by_core[:, core].reshape(768, 128).T
    for part in range(2):
        for way in range(2):
            @pl.when(line_sends(way, 0))
            def _():
                line_copy(way, 0, part).start()

    load_stream(0).wait()
    values = second[...].astype(F32)
    center = values - jnp.mean(values, axis=-1, keepdims=True)
    inv_std = lax.rsqrt(jnp.mean(center * center, axis=-1, keepdims=True) + EPSILON)
    unit[...] = center * inv_std
    spread_std[...] = jnp.broadcast_to(inv_std, (128, 128))
    unit_b = unit[...].astype(BF16)
    for i in range(8):
        lhs[i] = unit_b[:, 192 * i:192 * i + 192]

    @pl.when((c == 1) & jnp.logical_not(edge))
    def _():
        near_copy(0).wait_recv()
        begin_far(0)

    def finish(m):
        proj[m] = acc[m].T.astype(BF16).reshape(4, 192, 128)
        for d in range(1, 4):
            spread_copy(m, d).start()
        recv[m, 2 + zl] = proj[m, zl]

    def gather_step(t, _):
        def at(late, f, s, last=OUT):
            m = t - late - s

            @pl.when((m >= 0) & (m <= last))
            def _():
                f(m, s)

        for s in (3, 2, 1, 0):
            at(0, ring_step, s)
        for s in (3, 2, 1, 0):
            at(1, cross_step, s)

        @pl.when(t < 3)
        def _():
            have_own(t + 1)
            inner_far(t + 1)

            @pl.when(c == 1)
            def _():
                begin_far(t + 1)

        @pl.when(t < 6)
        def _():
            line_step(t // 2, t % 2)

        at(1, lambda m, s: have_far(m), 0)
        at(1, lambda m, s: project(m, y, True), 0, QUERY)
        for s in (3, 2, 1, 0):
            at(1, project_step, s)
        at(4, lambda m, s: finish(m), 0, QUERY)

        @pl.when(t == 6)
        def _():
            other_half().start()

        @pl.when(t >= 6)
        def _():
            m = t - 6
            for d in range(1, 4):
                spread_arrived(m, d).wait_recv()
            for way in range(2):
                halo_copy(m, way).start()

        return 0

    lax.fori_loop(0, 8, gather_step, 0)

    columns = pl.ds(pl.multiple_of((zl // 2) * 384, 128), 384)
    dm_all[...] = sum(
        nn(up_all[:, core].reshape(512, 768), wall[OUT, :, :, core, :, columns].reshape(768, 384))
        for core in range(2)).T.astype(BF16)
    dm[...] = dm_all[pl.ds(pl.multiple_of((zl % 2) * 192, 64), 192), :]

    for m in (KEY, VALUE):
        for way in range(2):
            halo_copy(m, way).wait_recv()
    for e in range(8):
        for m, natural, turned in ((KEY, kn, kt), (VALUE, vn, vt)):
            block = recv[m, e]
            flat = block.T
            for h in range(3):
                turned[h, :, 128 * e:128 * e + 128] = block[64 * h:64 * h + 64]
                natural[h, 128 * e:128 * e + 128, :] = flat[:, 64 * h:64 * h + 64]

    scale = HDIM ** -0.5
    dkv[...] = jnp.zeros_like(dkv)

    def window(j):
        return pl.ds(pl.multiple_of(j * 128, 128), 640)

    def of_block(j):
        return pl.ds(pl.multiple_of(j * 128, 128), 128)

    def forward(i, _):
        j = (zl + 4 - i) % 4

        @pl.when(i > 0)
        def _():
            spread_arrived(QUERY, i).wait_recv()

        for h in range(3):
            rows = slice(64 * h, 64 * h + 64)
            scores = nn(kn[h, window(j), :], recv[QUERY, 2 + j, rows, :] * scale)
            exps = jnp.exp(scores - jnp.max(scores, axis=0, keepdims=True))
            weights = (exps * (1 / jnp.sum(exps, axis=0, keepdims=True))).astype(BF16)
            probs[j, h] = weights
            mix[j, rows, :] = nn(vt[h, :, window(j)], weights).astype(BF16)
            dkv[1, h, :, window(j)] += nt(dm[rows, of_block(j)], weights)
        other_mix(j).start()
        send_back(MIX, mix.at[j], j)
        return 0

    def backward(j, _):
        for h in range(3):
            rows = slice(64 * h, 64 * h + 64)
            dmh = dm[rows, of_block(j)] * scale
            delta = jnp.sum(dmh.astype(F32) * mix[j, rows, :].astype(F32), axis=0, keepdims=True)
            d_weights = nn(vn[h, window(j), :], dmh)
            d_scores = (probs[j, h].astype(F32) * (d_weights - delta)).astype(BF16)
            dq[j, rows, :] = nn(kt[h, :, window(j)], d_scores).astype(BF16)
            dkv[0, h, :, window(j)] += nt(recv[QUERY, 2 + j, rows, :], d_scores)
        send_back(DQ, dq.at[j], j)
        return 0

    def send_halo(kv, way):
        lanes = slice(0, 256) if way == 0 else slice(768, 1024)
        halo_out[kv, way] = dkv[kv, :, :, lanes].astype(BF16).reshape(192, 256)
        ghalo_copy(kv, way).start()

    def finish_halo(kv):
        for way in range(2):
            ghalo_copy(kv, way).wait_recv()
            for i in range(2):
                j = i + 2 - 2 * way
                got = halo_in[kv, way, :, 128 * i:128 * i + 128].astype(F32)
                own = dkv[kv, :, :, 256 + 128 * j:384 + 128 * j].reshape(192, 128)
                dkv_out[kv, j] = (own + got).astype(BF16)
                send_back(DK + kv, dkv_out.at[kv, j], j)

    lax.fori_loop(0, 4, forward, 0)
    for way in range(2):
        send_halo(1, way)
    lax.fori_loop(0, 2, backward, 0)
    send_halo(0, 0)

    other_half().wait_recv()
    for j in range(4):
        other_mix(j).wait_recv()
    rows = sum(
        nn(jnp.concatenate([mix[j], mix_other[j]], axis=1),
           jnp.concatenate([up_all[j, c], up_other[j]], axis=0)) for j in range(4))
    xs[...] = rows.astype(BF16).reshape(4, 48, 768)
    for d in range(1, 4):
        x_copy(d).start()

    lax.fori_loop(2, 4, backward, 0)
    send_halo(0, 1)
    finish_halo(1)

    def drain(m, _):
        @pl.when(edge & (c == parity))
        def _():
            far_copy(m).wait_send()

        @pl.when(edge & (c == 1))
        def _():
            near_copy(m).wait_send()

        @pl.when(c == 1)
        def _():
            cross_far(m).wait_send()
            for kind in range(2):
                core_far(m, kind).wait_send()

        core_own(m, c).wait_send()
        for s in range(4):
            for way in ways_of(s):
                if s < 3:
                    ring_copy(m, way, s).wait_send()
                else:
                    ring_last(m).wait_send()
                cross_copy(m, way, s).wait_send()
                for kind in range(2):
                    core_copy(m, kind, way, s).wait_send()
        for d in range(1, 4):
            @pl.when(m < OUT)
            def _():
                spread_copy(m, d).wait_send()

        return 0

    def natural(t):
        return back[t].reshape(768, 128).T

    lax.fori_loop(0, 4, drain, 0)

    for d in range(1, 4):
        x_copy(d).wait_recv()
    part = xs[x].astype(F32)
    for d in range(3):
        part = part + xr[d].astype(F32)
    for i in range(8):
        ys[i] = part[:, 96 * i:96 * i + 96].astype(BF16)
    for d in range(1, 8):
        y_copy(d).start()

    finish_halo(0)

    wait_back(MIX)
    load_stream(2).wait()
    mixture = natural(MIX)
    for i in range(4):
        lanes = slice(384 * i, 384 * i + 384)
        branch = nt(mixture, wall[OUT, 2 * i:2 * i + 2].reshape(384, 768))
        x_ref[0, :, lanes] = (first[:, lanes].astype(F32) - branch).astype(BF16)

    def add_unit(t, m, first=False):
        wait_back(t)
        grads = natural(t)
        for i in range(4):
            lanes = slice(384 * i, 384 * i + 384)
            term = nt(grads, wall[m, 2 * i:2 * i + 2].reshape(384, 768))
            if first:
                d_unit[:, lanes] = term
            else:
                d_unit[:, lanes] += term

    add_unit(DQ, QUERY, True)
    add_unit(DV, VALUE)

    for d in range(1, 8):
        y_copy(d).wait_recv()
    part = ys[y].astype(F32)
    for d in range(7):
        part = part + yr[d].astype(F32)
    for i in range(2):
        fs[i] = part[:, 48 * i:48 * i + 48]
    far_piece().start()

    @pl.when(x != zl)
    def _():
        here_copy().start()

    @pl.when(x == zl)
    def _():
        fr[0] = fs[zh]

    add_unit(DK, KEY)
    grads = d_unit[...]
    kept = unit[...]
    correction = (grads - jnp.mean(grads, axis=-1, keepdims=True)
                  - kept * jnp.mean(grads * kept, axis=-1, keepdims=True))
    load_stream(3).wait()
    dx_ref[0] = (dsecond[...].astype(F32) + spread_std[:, :1] * correction).astype(BF16)

    far_piece().wait_recv()

    @pl.when(x != zl)
    def _():
        here_copy().wait_recv()

    grad_ref[...] = (fr[0] + fr[1]) / 32

    for kv in range(2):
        for way in range(2):
            halo_copy(kv, way).wait_send()
            ghalo_copy(kv, way).wait_send()
    other_half().wait_send()
    for j in range(4):
        other_mix(j).wait_send()
    for t in (MIX, DQ, DK, DV):
        for d in range(1, 4):
            g = (zl + d) % 4
            back_copy(t, mix.at[g], g).wait_send()
    for d in range(1, 4):
        x_copy(d).wait_send()
    for d in range(1, 8):
        y_copy(d).wait_send()
    far_piece().wait_send()

    @pl.when(x != zl)
    def _():
        here_copy().wait_send()

    for way in range(2):
        for k in range(3):
            @pl.when(line_sends(way, k))
            def _():
                for part in range(2):
                    line_copy(way, k, part).wait_send()


def block(y_first, y_second, upstream, dy_second, in_proj, out_t):
    vmem = pl.BlockSpec(memory_space=pltpu.VMEM)
    dma = pltpu.SemaphoreType.DMA
    stream = jax.ShapeDtypeStruct((1, 128, 1536), BF16)
    return pl.pallas_call(
        kernel,
        out_shape=(stream, stream, jax.ShapeDtypeStruct((48, 48), F32)),
        in_specs=[pl.BlockSpec(memory_space=pl.ANY)] * 6,
        out_specs=(vmem,) * 3,
        scratch_shapes=[
            pltpu.VMEM((128, 1536), BF16),
            pltpu.VMEM((128, 1536), BF16),
            pltpu.VMEM((128, 1536), BF16),
            pltpu.VMEM((128, 1536), BF16),
            pltpu.VMEM((128, 1536), F32),
            pltpu.VMEM((128, 128), F32),
            pltpu.VMEM((4, 8, 2, 2, 48, 768), BF16),
            pltpu.VMEM((8, 128, 192), BF16),
            pltpu.VMEM((3, 128, 768), F32),
            pltpu.VMEM((3, 4, 192, 128), BF16),
            pltpu.VMEM((3, 8, 192, 128), BF16),
            pltpu.VMEM((3, 1024, 64), BF16),
            pltpu.VMEM((3, 1024, 64), BF16),
            pltpu.VMEM((3, 64, 1024), BF16),
            pltpu.VMEM((3, 64, 1024), BF16),
            pltpu.VMEM((4, 3, 640, 128), BF16),
            pltpu.VMEM((4, 192, 128), BF16),
            pltpu.VMEM((4, 192, 128), BF16),
            pltpu.VMEM((2, 3, 64, 1024), F32),
            pltpu.VMEM((2, 2, 192, 256), BF16),
            pltpu.VMEM((2, 2, 192, 256), BF16),
            pltpu.VMEM((2, 4, 192, 128), BF16),
            pltpu.VMEM((4, 4, 192, 128), BF16),
            pltpu.VMEM((128, 1536), F32),
            pltpu.VMEM((4, 2, 128, 768), BF16),
            pltpu.VMEM((4, 128, 768), BF16),
            pltpu.VMEM((4, 192, 128), BF16),
            pltpu.VMEM((384, 512), BF16),
            pltpu.VMEM((192, 512), BF16),
            pltpu.VMEM((4, 48, 768), BF16),
            pltpu.VMEM((3, 48, 768), BF16),
            pltpu.VMEM((8, 48, 96), BF16),
            pltpu.VMEM((7, 48, 96), BF16),
            pltpu.VMEM((2, 48, 48), F32),
            pltpu.VMEM((2, 48, 48), F32),
            dma((4,)), dma((4,)),
            dma((4,)), dma((4,)), dma((4,)),
            dma((4, 7)), dma((4, 7)),
            dma((4, 8)), dma((4, 8)),
            dma((4, 2, 9)), dma((4, 2, 9)),
            dma((2, 3, 2)), dma((2, 3, 2)),
            dma((5,)), dma((5,)),
            dma((3, 3)), dma((3, 3)),
            dma((2, 2)), dma((2, 2)),
            dma((2, 2)), dma((2, 2)),
            dma((4, 4)), dma((4, 4)),
            dma((3,)), dma((3,)),
            dma((7,)), dma((7,)),
            dma((2,)), dma((2,)),
        ],
        compiler_params=pltpu.CompilerParams(
            collective_id=0, has_side_effects=True, vmem_limit_bytes=62 * 2**20),
        name="attention_block_backward",
    )(y_first, y_second, upstream, dy_second, in_proj, out_t)


def body(y_first, y_second, first_output_cotangent, dy_second, in_proj, out_proj):
    return block(y_first, y_second, first_output_cotangent, dy_second, in_proj, out_proj.T)


def solution(mesh):
    placed = (
        P("wide", "blk", None),
        P("wide", "blk", None),
        P("wide", "blk", None),
        P("wide", "blk", None),
        P(None, "wide", None),
        P(None, "wide"),
    )
    return jax.shard_map(
        body,
        mesh=mesh,
        in_specs=placed,
        out_specs=(P("wide", "blk", None), P("wide", "blk", None), P("blk", "wide")),
        check_vma=False,
    )
```

```python
import functools

import jax
import jax.numpy as jnp
from jax import lax
from jax.experimental import pallas as pl
from jax.experimental.pallas import tpu as pltpu
from jax.sharding import PartitionSpec as P

HDIM = 64
EPSILON = 1e-05
MESH = pl.DeviceIdType.MESH
F32 = jnp.float32
BF16 = jnp.bfloat16

KEY, VALUE, QUERY, OUT = range(4)
MIX, DQ, DK, DV = range(4)


def nt(a, b):
    return lax.dot_general(a, b, (((1,), (1,)), ((), ())), preferred_element_type=F32)


def nn(a, b):
    return jnp.dot(a, b, preferred_element_type=F32)


def kernel(first_ref, second_ref, upstream_ref, dsecond_ref, in_ref, out_ref,
           x_ref, dx_ref, grad_ref,
           first, second, upstream_in, dsecond, unit, spread_std, wall, lhs, acc, proj, recv, kn, vn, kt, vt, probs, mix, dq, dkv, halo_out,
           halo_in, dkv_out, back, d_unit, up_all, up_other, mix_other, dm_all, dm, xs, xr, ys, yr,
           fs, fr,
           load_sem, stream_sem, far_send, near_send, far_recv, ring_send, ring_recv,
           cross_send, cross_recv, core_send, core_recv,
           line_send, line_recv, swap_send, swap_recv, spread_send, spread_recv, halo_send, halo_recv,
           ghalo_send, ghalo_recv, back_send, back_recv,
           xs_send, xs_recv, ys_send, ys_recv, fs_send, fs_recv):
    b, w = lax.axis_index("blk"), lax.axis_index("wide")
    x, zl, y, zh, c = b // 4, b % 4, w // 4, (w // 2) % 2, w % 2
    edge = (zl == 0) | (zl == 3)
    half = (zh, 1 - zh)
    carried, parity = (zh + c) % 2, x % 2

    def at_x(d):
        return {"blk": ((x + d) % 4) * 4 + zl}

    def at_y(d):
        return {"wide": ((y + d) % 8) * 4 + zh * 2 + c}

    def at_z(d):
        return {"blk": x * 4 + (zl + d) % 4}

    above, below = at_y(1), at_y(7)
    partner = {"wide": w + 1 - 2 * c}
    crosses = edge & ((parity == 0) | (c == 1))
    far = {"blk": b + 3 - 2 * zl,
           "wide": y * 4 + (1 - zh) * 2 + jnp.where(parity == 0, 1 - c, c)}
    near = {"blk": b + 1 - 2 * (b % 2)}

    def copy(src, dst, send, got, device):
        return pltpu.make_async_remote_copy(
            src_ref=src, dst_ref=dst, send_sem=send, recv_sem=got,
            device_id=device, device_id_type=MESH)

    barrier = pltpu.get_barrier_semaphore()
    greeted = [partner] + [at_x(d) for d in range(1, 4)] + [at_y(d) for d in range(1, 8)]
    greeted += [at_z(d) for d in range(1, 4)]
    turned_here = {"blk": zl * 4 + x}
    turned_far = {"blk": zl * 4 + x, "wide": w + 2 - 4 * zh}
    for device in greeted:
        pl.semaphore_signal(barrier, inc=1, device_id=device, device_id_type=MESH)

    @pl.when(crosses)
    def _():
        pl.semaphore_signal(barrier, inc=1, device_id=far, device_id_type=MESH)

    pl.semaphore_signal(barrier, inc=1, device_id=turned_far, device_id_type=MESH)

    @pl.when(x != zl)
    def _():
        pl.semaphore_signal(barrier, inc=1, device_id=turned_here, device_id_type=MESH)

    def load_weight(m):
        source = (in_ref.at[1], in_ref.at[2], in_ref.at[0], out_ref)[m]
        return pltpu.make_async_copy(source, wall.at[m, y, zh, c], load_sem.at[m])

    streams = ((second_ref, second), (upstream_ref, upstream_in), (first_ref, first),
               (dsecond_ref, dsecond))

    def load_stream(i):
        return pltpu.make_async_copy(streams[i][0].at[0], streams[i][1], stream_sem.at[i])

    for m in range(4):
        load_weight(m).start()
    for i in range(4):
        load_stream(i).start()
    for m in range(4):
        load_weight(m).wait()
    extra = 1 + crosses.astype(jnp.int32) + (x != zl).astype(jnp.int32)
    pl.semaphore_wait(barrier, len(greeted) + extra)

    def far_copy(m):
        block = wall.at[m, y, zh, c]
        return copy(block, block, far_send.at[m], far_recv.at[m], far)

    def near_copy(m):
        block = wall.at[m, y, 1 - zh, parity]
        return copy(block, block, near_send.at[m], far_recv.at[m], near)

    def place(way, s):
        return (y + 7 - s) % 8 if way == 0 else (y + 1 + s) % 8

    def slot(way, s):
        return s if way == 0 else 4 + s

    def ring_copy(m, way, s):
        origin = (y + 8 - s) % 8 if way == 0 else (y + s) % 8
        block = wall.at[m, origin, carried, parity]
        j = slot(way, s)
        return copy(block, block, ring_send.at[m, j], ring_recv.at[m, j],
                    above if way == 0 else below)

    def ring_got(m, way, s):
        block = wall.at[m, place(way, s), carried, parity]
        j = slot(way, s)
        return copy(block, block, ring_send.at[m, j], ring_recv.at[m, j], above)

    def ring_last(m):
        block = wall.at[m, (y + 5 + 6 * c) % 8, carried, parity]
        return copy(block, block, ring_send.at[m, 3], ring_recv.at[m, 3],
                    {"wide": ((y + 1 + 6 * c) % 8) * 4 + zh * 2 + c})

    def cross_copy(m, way, s):
        block = wall.at[m, place(way, s), carried, parity]
        j = slot(way, s)
        to = 1 + 2 * c if s == 3 else (1, 3)[way]
        return copy(block, block, cross_send.at[m, j], cross_recv.at[m, j], at_x(to))

    def cross_got(m, way, s):
        block = wall.at[m, place(way, s), carried, 1 - parity]
        j = slot(way, s)
        return copy(block, block, cross_send.at[m, j], cross_recv.at[m, j], at_x(1))

    def core_copy(m, kind, way, s, mine=True):
        half_of = carried if mine else 1 - carried
        block = wall.at[m, place(way, s), half_of, 1 - parity if kind else parity]
        j = slot(way, s)
        return copy(block, block, core_send.at[m, kind, j], core_recv.at[m, kind, j], partner)

    def core_own(m, core):
        block = wall.at[m, y, zh, core]
        return copy(block, block, core_send.at[m, 0, 7], core_recv.at[m, 0, 7], partner)

    def core_far(m, kind):
        block = wall.at[m, y, 1 - zh, 1 - parity if kind else parity]
        return copy(block, block, core_send.at[m, 1, 7 + kind], core_recv.at[m, 1, 7 + kind],
                    partner)

    def cross_far(m, own=True):
        block = wall.at[m, y, 1 - zh, parity if own else 1 - parity]
        return copy(block, block, cross_send.at[m, 7], cross_recv.at[m, 7], at_x(1))

    def ways_of(s):
        return (0, 1) if s < 3 else (0,)

    def start_stream(m):
        for way in range(2):
            ring_copy(m, way, 0).start()

    def have_own(m):
        core_own(m, 1 - c).wait_recv()

        @pl.when(c == 0)
        def _():
            start_stream(m)

    def begin_far(m):
        start_stream(m)
        core_far(m, 0).start()
        cross_far(m).start()

    def inner_far(m):
        @pl.when((c == 1) & jnp.logical_not(edge))
        def _():
            near_copy(m).wait_recv()

    def have_far(m):
        @pl.when(c == 1)
        def _():
            cross_far(m, False).wait_recv()
            core_far(m, 1).start()

        @pl.when(c == 0)
        def _():
            core_far(m, 0).wait_recv()
            core_far(m, 1).wait_recv()

    def ring_step(m, s):
        for way in ways_of(s):
            ring_got(m, way, s).wait_recv()
            if s < 2:
                ring_copy(m, way, s + 1).start()
            if s == 2:
                @pl.when(c == way)
                def _():
                    ring_last(m).start()
            cross_copy(m, way, s).start()
            core_copy(m, 0, way, s).start()

    def cross_step(m, s):
        for way in ways_of(s):
            cross_got(m, way, s).wait_recv()
            core_copy(m, 1, way, s).start()

    def project(m, origin, first=False):
        term = nn(lhs[origin], wall[m, origin].reshape(192, 768))
        if first:
            acc[m] = term
        else:
            acc[m] += term

    def project_step(m, s):
        for way in ways_of(s):
            for kind in range(2):
                core_copy(m, kind, way, s, False).wait_recv()

            @pl.when(m < OUT)
            def _():
                project(m, place(way, s))

    def spread_copy(m, d):
        return copy(proj.at[m, (zl + d) % 4], recv.at[m, 2 + zl], spread_send.at[m, d - 1],
                    spread_recv.at[m, d - 1], at_z(d))

    def spread_arrived(m, d):
        return copy(proj.at[m, (zl + d) % 4], recv.at[m, 2 + (zl + 4 - d) % 4],
                    spread_send.at[m, d - 1], spread_recv.at[m, d - 1], at_z(d))

    def halo_copy(m, way, arriving=False):
        start = (4, 2)[way]
        into = (0, 6)[way]
        return copy(recv.at[m, start:start + 2], recv.at[m, into:into + 2],
                    halo_send.at[m, way], halo_recv.at[m, way], at_x((1, 3)[way]))

    def ghalo_copy(kv, way):
        return copy(halo_out.at[kv, way], halo_in.at[kv, way], ghalo_send.at[kv, way],
                    ghalo_recv.at[kv, way], at_x((3, 1)[way]))

    def back_copy(t, source, j):
        return copy(source, back.at[t, zl], back_send.at[t, j], back_recv.at[t, zl],
                    {"blk": x * 4 + j})

    def send_back(t, source, j):
        @pl.when(j != zl)
        def _():
            back_copy(t, source, j).start()

        @pl.when(j == zl)
        def _():
            back[t, zl] = source[...]

    def wait_back(t):
        for d in range(1, 4):
            g = (zl + d) % 4
            copy(back.at[t, g], back.at[t, g], back_send.at[t, g], back_recv.at[t, g],
                 {"blk": x * 4 + g}).wait_recv()

    def line_sends(way, k):
        return (zl < 3) & (zl >= k) if way == 0 else (zl > 0) & (zl + k <= 3)

    def line_gets(way, k):
        return zl >= k + 1 if way == 0 else zl + k <= 2

    def line_copy(way, k, part):
        block = up_all.at[zl - k if way == 0 else zl + k, part]
        return copy(block, block, line_send.at[way, k, part], line_recv.at[way, k, part],
                    {"blk": b + 1 if way == 0 else b - 1})

    def line_got(way, k, part):
        block = up_all.at[zl - 1 - k if way == 0 else zl + 1 + k, part]
        return copy(block, block, line_send.at[way, k, part], line_recv.at[way, k, part],
                    {"blk": b + 1 if way == 0 else b - 1})

    def line_step(k, part):
        for way in range(2):
            @pl.when(line_gets(way, k))
            def _():
                line_got(way, k, part).wait_recv()

                @pl.when(line_sends(way, k + 1))
                def _():
                    line_copy(way, k + 1, part).start()

    def other_half():
        return copy(up_all.at[:, 1 - c], up_other, swap_send.at[0], swap_recv.at[0], partner)

    def other_mix(j):
        return copy(mix.at[j], mix_other.at[j], swap_send.at[1 + j], swap_recv.at[1 + j], partner)

    def x_copy(d):
        return copy(xs.at[(x + d) % 4], xr.at[d - 1], xs_send.at[d - 1], xs_recv.at[d - 1], at_x(d))

    def y_copy(d):
        return copy(ys.at[(y + d) % 8], yr.at[d - 1], ys_send.at[d - 1], ys_recv.at[d - 1], at_y(d))

    def here_copy():
        return copy(fs.at[zh], fr.at[0], fs_send.at[0], fs_recv.at[0], turned_here)

    def far_piece():
        return copy(fs.at[1 - zh], fr.at[1], fs_send.at[1], fs_recv.at[1], turned_far)

    @pl.when(edge & (c == parity))
    def _():
        for m in range(4):
            far_copy(m).start()

    for m in range(4):
        core_own(m, c).start()
    have_own(0)

    @pl.when(edge & (c == 1))
    def _():
        for m in range(4):
            near_copy(m).wait_recv()
            near_copy(m).start()
            if m == 0:
                begin_far(0)

    load_stream(1).wait()
    by_core = upstream_in[...].T.reshape(16, 2, 48, 128)
    for core in range(2):
        up_all[zl, core] = by_core[:, core].reshape(768, 128).T
    for part in range(2):
        for way in range(2):
            @pl.when(line_sends(way, 0))
            def _():
                line_copy(way, 0, part).start()

    load_stream(0).wait()
    values = second[...].astype(F32)
    center = values - jnp.mean(values, axis=-1, keepdims=True)
    inv_std = lax.rsqrt(jnp.mean(center * center, axis=-1, keepdims=True) + EPSILON)
    unit[...] = center * inv_std
    spread_std[...] = jnp.broadcast_to(inv_std, (128, 128))
    unit_b = unit[...].astype(BF16)
    for i in range(8):
        lhs[i] = unit_b[:, 192 * i:192 * i + 192]

    @pl.when((c == 1) & jnp.logical_not(edge))
    def _():
        near_copy(0).wait_recv()
        begin_far(0)

    def finish(m):
        proj[m] = acc[m].T.astype(BF16).reshape(4, 192, 128)
        for d in range(1, 4):
            spread_copy(m, d).start()
        recv[m, 2 + zl] = proj[m, zl]

    def gather_step(t, _):
        def at(late, f, s, last=OUT):
            m = t - late - s

            @pl.when((m >= 0) & (m <= last))
            def _():
                f(m, s)

        for s in (3, 2, 1, 0):
            at(0, ring_step, s)
        for s in (3, 2, 1, 0):
            at(1, cross_step, s)

        @pl.when(t < 3)
        def _():
            have_own(t + 1)
            inner_far(t + 1)

            @pl.when(c == 1)
            def _():
                begin_far(t + 1)

        @pl.when(t < 6)
        def _():
            line_step(t // 2, t % 2)

        at(1, lambda m, s: have_far(m), 0)
        at(1, lambda m, s: project(m, y, True), 0, QUERY)
        for s in (3, 2, 1, 0):
            at(1, project_step, s)
        at(4, lambda m, s: finish(m), 0, QUERY)

        @pl.when(t == 6)
        def _():
            other_half().start()

        @pl.when(t >= 6)
        def _():
            m = t - 6
            for d in range(1, 4):
                spread_arrived(m, d).wait_recv()
            for way in range(2):
                halo_copy(m, way).start()

        return 0

    lax.fori_loop(0, 8, gather_step, 0)

    columns = pl.ds(pl.multiple_of((zl // 2) * 384, 128), 384)
    dm_all[...] = sum(
        nn(up_all[:, core].reshape(512, 768), wall[OUT, :, :, core, :, columns].reshape(768, 384))
        for core in range(2)).T.astype(BF16)
    dm[...] = dm_all[pl.ds(pl.multiple_of((zl % 2) * 192, 64), 192), :]

    for m in (KEY, VALUE):
        for way in range(2):
            halo_copy(m, way).wait_recv()
    for e in range(8):
        for m, natural, turned in ((KEY, kn, kt), (VALUE, vn, vt)):
            block = recv[m, e]
            flat = block.T
            for h in range(3):
                turned[h, :, 128 * e:128 * e + 128] = block[64 * h:64 * h + 64]
                natural[h, 128 * e:128 * e + 128, :] = flat[:, 64 * h:64 * h + 64]

    scale = HDIM ** -0.5
    dkv[...] = jnp.zeros_like(dkv)

    def window(j):
        return pl.ds(pl.multiple_of(j * 128, 128), 640)

    def of_block(j):
        return pl.ds(pl.multiple_of(j * 128, 128), 128)

    def forward(i, _):
        j = (zl + 4 - i) % 4

        @pl.when(i > 0)
        def _():
            spread_arrived(QUERY, i).wait_recv()

        for h in range(3):
            rows = slice(64 * h, 64 * h + 64)
            scores = nn(kn[h, window(j), :], recv[QUERY, 2 + j, rows, :] * scale)
            exps = jnp.exp(scores - jnp.max(scores, axis=0, keepdims=True))
            weights = (exps * (1 / jnp.sum(exps, axis=0, keepdims=True))).astype(BF16)
            probs[j, h] = weights
            mix[j, rows, :] = nn(vt[h, :, window(j)], weights).astype(BF16)
            dkv[1, h, :, window(j)] += nt(dm[rows, of_block(j)], weights)
        other_mix(j).start()
        send_back(MIX, mix.at[j], j)
        return 0

    def backward(j, _):
        for h in range(3):
            rows = slice(64 * h, 64 * h + 64)
            dmh = dm[rows, of_block(j)] * scale
            delta = jnp.sum(dmh.astype(F32) * mix[j, rows, :].astype(F32), axis=0, keepdims=True)
            d_weights = nn(vn[h, window(j), :], dmh)
            d_scores = (probs[j, h].astype(F32) * (d_weights - delta)).astype(BF16)
            dq[j, rows, :] = nn(kt[h, :, window(j)], d_scores).astype(BF16)
            dkv[0, h, :, window(j)] += nt(recv[QUERY, 2 + j, rows, :], d_scores)
        send_back(DQ, dq.at[j], j)
        return 0

    def send_halo(kv, way):
        lanes = slice(0, 256) if way == 0 else slice(768, 1024)
        halo_out[kv, way] = dkv[kv, :, :, lanes].astype(BF16).reshape(192, 256)
        ghalo_copy(kv, way).start()

    def finish_halo(kv):
        for way in range(2):
            ghalo_copy(kv, way).wait_recv()
            for i in range(2):
                j = i + 2 - 2 * way
                got = halo_in[kv, way, :, 128 * i:128 * i + 128].astype(F32)
                own = dkv[kv, :, :, 256 + 128 * j:384 + 128 * j].reshape(192, 128)
                dkv_out[kv, j] = (own + got).astype(BF16)
                send_back(DK + kv, dkv_out.at[kv, j], j)

    lax.fori_loop(0, 4, forward, 0)
    for way in range(2):
        send_halo(1, way)
    lax.fori_loop(0, 2, backward, 0)
    send_halo(0, 0)

    other_half().wait_recv()
    for j in range(4):
        other_mix(j).wait_recv()
    rows = sum(
        nn(jnp.concatenate([mix[j], mix_other[j]], axis=1),
           jnp.concatenate([up_all[j, c], up_other[j]], axis=0)) for j in range(4))
    xs[...] = rows.astype(BF16).reshape(4, 48, 768)
    for d in range(1, 4):
        x_copy(d).start()

    lax.fori_loop(2, 4, backward, 0)
    send_halo(0, 1)
    finish_halo(1)

    def drain(m, _):
        @pl.when(edge & (c == parity))
        def _():
            far_copy(m).wait_send()

        @pl.when(edge & (c == 1))
        def _():
            near_copy(m).wait_send()

        @pl.when(c == 1)
        def _():
            cross_far(m).wait_send()
            for kind in range(2):
                core_far(m, kind).wait_send()

        core_own(m, c).wait_send()
        for s in range(4):
            for way in ways_of(s):
                if s < 3:
                    ring_copy(m, way, s).wait_send()
                else:
                    ring_last(m).wait_send()
                cross_copy(m, way, s).wait_send()
                for kind in range(2):
                    core_copy(m, kind, way, s).wait_send()
        for d in range(1, 4):
            @pl.when(m < OUT)
            def _():
                spread_copy(m, d).wait_send()

        return 0

    def natural(t):
        return back[t].reshape(768, 128).T

    lax.fori_loop(0, 4, drain, 0)

    for d in range(1, 4):
        x_copy(d).wait_recv()
    part = xs[x].astype(F32)
    for d in range(3):
        part = part + xr[d].astype(F32)
    for i in range(8):
        ys[i] = part[:, 96 * i:96 * i + 96].astype(BF16)
    for d in range(1, 8):
        y_copy(d).start()

    finish_halo(0)

    wait_back(MIX)
    load_stream(2).wait()
    mixture = natural(MIX)
    for i in range(4):
        lanes = slice(384 * i, 384 * i + 384)
        branch = nt(mixture, wall[OUT, 2 * i:2 * i + 2].reshape(384, 768))
        x_ref[0, :, lanes] = (first[:, lanes].astype(F32) - branch).astype(BF16)

    def add_unit(t, m, first=False):
        wait_back(t)
        grads = natural(t)
        for i in range(4):
            lanes = slice(384 * i, 384 * i + 384)
            term = nt(grads, wall[m, 2 * i:2 * i + 2].reshape(384, 768))
            if first:
                d_unit[:, lanes] = term
            else:
                d_unit[:, lanes] += term

    add_unit(DQ, QUERY, True)
    add_unit(DV, VALUE)

    for d in range(1, 8):
        y_copy(d).wait_recv()
    part = ys[y].astype(F32)
    for d in range(7):
        part = part + yr[d].astype(F32)
    for i in range(2):
        fs[i] = part[:, 48 * i:48 * i + 48]
    far_piece().start()

    @pl.when(x != zl)
    def _():
        here_copy().start()

    @pl.when(x == zl)
    def _():
        fr[0] = fs[zh]

    add_unit(DK, KEY)
    grads = d_unit[...]
    kept = unit[...]
    correction = (grads - jnp.mean(grads, axis=-1, keepdims=True)
                  - kept * jnp.mean(grads * kept, axis=-1, keepdims=True))
    load_stream(3).wait()
    dx_ref[0] = (dsecond[...].astype(F32) + spread_std[:, :1] * correction).astype(BF16)

    far_piece().wait_recv()

    @pl.when(x != zl)
    def _():
        here_copy().wait_recv()

    grad_ref[...] = (fr[0] + fr[1]) / 32

    for kv in range(2):
        for way in range(2):
            halo_copy(kv, way).wait_send()
            ghalo_copy(kv, way).wait_send()
    other_half().wait_send()
    for j in range(4):
        other_mix(j).wait_send()
    for t in (MIX, DQ, DK, DV):
        for d in range(1, 4):
            g = (zl + d) % 4
            back_copy(t, mix.at[g], g).wait_send()
    for d in range(1, 4):
        x_copy(d).wait_send()
    for d in range(1, 8):
        y_copy(d).wait_send()
    far_piece().wait_send()

    @pl.when(x != zl)
    def _():
        here_copy().wait_send()

    for way in range(2):
        for k in range(3):
            @pl.when(line_sends(way, k))
            def _():
                for part in range(2):
                    line_copy(way, k, part).wait_send()


def block(y_first, y_second, upstream, dy_second, in_proj, out_t):
    vmem = pl.BlockSpec(memory_space=pltpu.VMEM)
    dma = pltpu.SemaphoreType.DMA
    stream = jax.ShapeDtypeStruct((1, 128, 1536), BF16)
    return pl.pallas_call(
        kernel,
        out_shape=(stream, stream, jax.ShapeDtypeStruct((48, 48), F32)),
        in_specs=[pl.BlockSpec(memory_space=pl.ANY)] * 6,
        out_specs=(vmem,) * 3,
        scratch_shapes=[
            pltpu.VMEM((128, 1536), BF16),
            pltpu.VMEM((128, 1536), BF16),
            pltpu.VMEM((128, 1536), BF16),
            pltpu.VMEM((128, 1536), BF16),
            pltpu.VMEM((128, 1536), F32),
            pltpu.VMEM((128, 128), F32),
            pltpu.VMEM((4, 8, 2, 2, 48, 768), BF16),
            pltpu.VMEM((8, 128, 192), BF16),
            pltpu.VMEM((3, 128, 768), F32),
            pltpu.VMEM((3, 4, 192, 128), BF16),
            pltpu.VMEM((3, 8, 192, 128), BF16),
            pltpu.VMEM((3, 1024, 64), BF16),
            pltpu.VMEM((3, 1024, 64), BF16),
            pltpu.VMEM((3, 64, 1024), BF16),
            pltpu.VMEM((3, 64, 1024), BF16),
            pltpu.VMEM((4, 3, 640, 128), BF16),
            pltpu.VMEM((4, 192, 128), BF16),
            pltpu.VMEM((4, 192, 128), BF16),
            pltpu.VMEM((2, 3, 64, 1024), F32),
            pltpu.VMEM((2, 2, 192, 256), BF16),
            pltpu.VMEM((2, 2, 192, 256), BF16),
            pltpu.VMEM((2, 4, 192, 128), BF16),
            pltpu.VMEM((4, 4, 192, 128), BF16),
            pltpu.VMEM((128, 1536), F32),
            pltpu.VMEM((4, 2, 128, 768), BF16),
            pltpu.VMEM((4, 128, 768), BF16),
            pltpu.VMEM((4, 192, 128), BF16),
            pltpu.VMEM((384, 512), BF16),
            pltpu.VMEM((192, 512), BF16),
            pltpu.VMEM((4, 48, 768), BF16),
            pltpu.VMEM((3, 48, 768), BF16),
            pltpu.VMEM((8, 48, 96), BF16),
            pltpu.VMEM((7, 48, 96), BF16),
            pltpu.VMEM((2, 48, 48), F32),
            pltpu.VMEM((2, 48, 48), F32),
            dma((4,)), dma((4,)),
            dma((4,)), dma((4,)), dma((4,)),
            dma((4, 7)), dma((4, 7)),
            dma((4, 8)), dma((4, 8)),
            dma((4, 2, 9)), dma((4, 2, 9)),
            dma((2, 3, 2)), dma((2, 3, 2)),
            dma((5,)), dma((5,)),
            dma((3, 3)), dma((3, 3)),
            dma((2, 2)), dma((2, 2)),
            dma((2, 2)), dma((2, 2)),
            dma((4, 4)), dma((4, 4)),
            dma((3,)), dma((3,)),
            dma((7,)), dma((7,)),
            dma((2,)), dma((2,)),
        ],
        compiler_params=pltpu.CompilerParams(
            collective_id=0, has_side_effects=True, vmem_limit_bytes=62 * 2**20),
        name="attention_block_backward",
    )(y_first, y_second, upstream, dy_second, in_proj, out_t)


def hand_over(x_ref, dx_ref, grad_ref, x_out, dx_out, grad_out):
    x_out[...] = x_ref[...]
    dx_out[...] = dx_ref[...]
    grad_out[...] = grad_ref[...]


def body(y_first, y_second, first_output_cotangent, dy_second, in_proj, out_proj):
    made = block(y_first, y_second, first_output_cotangent, dy_second, in_proj, out_proj.T)
    vmem = pl.BlockSpec(memory_space=pltpu.VMEM)
    return pl.pallas_call(
        hand_over,
        out_shape=tuple(jax.ShapeDtypeStruct(a.shape, a.dtype) for a in made),
        in_specs=[vmem] * 3,
        out_specs=(vmem,) * 3,
        name="hand_over",
    )(*made)


def solution(mesh):
    placed = (
        P("wide", "blk", None),
        P("wide", "blk", None),
        P("wide", "blk", None),
        P("wide", "blk", None),
        P(None, "wide", None),
        P(None, "wide"),
    )
    return jax.shard_map(
        body,
        mesh=mesh,
        in_specs=placed,
        out_specs=(P("wide", "blk", None), P("wide", "blk", None), P("blk", "wide")),
        check_vma=False,
    )
```

```python
import functools

import jax
import jax.numpy as jnp
from jax import lax
from jax.experimental import pallas as pl
from jax.experimental.pallas import tpu as pltpu
from jax.sharding import PartitionSpec as P

HDIM = 64
EPSILON = 1e-05
MESH = pl.DeviceIdType.MESH
F32 = jnp.float32
BF16 = jnp.bfloat16

KEY, VALUE, QUERY, OUT = range(4)
MIX, DQ, DK, DV = range(4)


def nt(a, b):
    return lax.dot_general(a, b, (((1,), (1,)), ((), ())), preferred_element_type=F32)


def nn(a, b):
    return jnp.dot(a, b, preferred_element_type=F32)


def kernel(first_ref, second_ref, upstream_ref, dsecond_ref, in_ref, out_ref,
           x_ref, dx_ref, grad_ref,
           first, second, upstream_in, dsecond, unit, spread_std, wall, lhs, acc, proj, recv, kn, vn, kt, vt, probs, mix, dq, dkv, halo_out,
           halo_in, dkv_out, back, d_unit, up_all, up_other, mix_other, dm_all, dm, xs, xr, ys, yr,
           fs, fr,
           load_sem, stream_sem, far_send, near_send, far_recv, ring_send, ring_recv,
           cross_send, cross_recv, core_send, core_recv,
           line_send, line_recv, swap_send, swap_recv, spread_send, spread_recv, halo_send, halo_recv,
           ghalo_send, ghalo_recv, back_send, back_recv,
           xs_send, xs_recv, ys_send, ys_recv, fs_send, fs_recv):
    b, w = lax.axis_index("blk"), lax.axis_index("wide")
    x, zl, y, zh, c = b // 4, b % 4, w // 4, (w // 2) % 2, w % 2
    edge = (zl == 0) | (zl == 3)
    half = (zh, 1 - zh)
    carried, parity = (zh + c) % 2, x % 2

    def at_x(d):
        return {"blk": ((x + d) % 4) * 4 + zl}

    def at_y(d):
        return {"wide": ((y + d) % 8) * 4 + zh * 2 + c}

    def at_z(d):
        return {"blk": x * 4 + (zl + d) % 4}

    above, below = at_y(1), at_y(7)
    partner = {"wide": w + 1 - 2 * c}
    crosses = edge & ((parity == 0) | (c == 1))
    far = {"blk": b + 3 - 2 * zl,
           "wide": y * 4 + (1 - zh) * 2 + jnp.where(parity == 0, 1 - c, c)}
    near = {"blk": b + 1 - 2 * (b % 2)}

    def copy(src, dst, send, got, device):
        return pltpu.make_async_remote_copy(
            src_ref=src, dst_ref=dst, send_sem=send, recv_sem=got,
            device_id=device, device_id_type=MESH)

    barrier = pltpu.get_barrier_semaphore()
    greeted = [partner] + [at_x(d) for d in range(1, 4)] + [at_y(d) for d in range(1, 8)]
    greeted += [at_z(d) for d in range(1, 4)]
    turned_here = {"blk": zl * 4 + x}
    turned_far = {"blk": zl * 4 + x, "wide": w + 2 - 4 * zh}
    for device in greeted:
        pl.semaphore_signal(barrier, inc=1, device_id=device, device_id_type=MESH)

    @pl.when(crosses)
    def _():
        pl.semaphore_signal(barrier, inc=1, device_id=far, device_id_type=MESH)

    pl.semaphore_signal(barrier, inc=1, device_id=turned_far, device_id_type=MESH)

    @pl.when(x != zl)
    def _():
        pl.semaphore_signal(barrier, inc=1, device_id=turned_here, device_id_type=MESH)

    def load_weight(m):
        source = (in_ref.at[1], in_ref.at[2], in_ref.at[0], out_ref)[m]
        return pltpu.make_async_copy(source, wall.at[m, y, zh, c], load_sem.at[m])

    streams = ((second_ref, second), (upstream_ref, upstream_in), (first_ref, first),
               (dsecond_ref, dsecond))

    def load_stream(i):
        return pltpu.make_async_copy(streams[i][0].at[0], streams[i][1], stream_sem.at[i])

    for m in range(4):
        load_weight(m).start()
    for i in range(4):
        load_stream(i).start()
    for m in range(4):
        load_weight(m).wait()
    extra = 1 + crosses.astype(jnp.int32) + (x != zl).astype(jnp.int32)
    pl.semaphore_wait(barrier, len(greeted) + extra)

    def far_copy(m):
        block = wall.at[m, y, zh, c]
        return copy(block, block, far_send.at[m], far_recv.at[m], far)

    def near_copy(m):
        block = wall.at[m, y, 1 - zh, parity]
        return copy(block, block, near_send.at[m], far_recv.at[m], near)

    def place(way, s):
        return (y + 7 - s) % 8 if way == 0 else (y + 1 + s) % 8

    def slot(way, s):
        return s if way == 0 else 4 + s

    def ring_copy(m, way, s):
        origin = (y + 8 - s) % 8 if way == 0 else (y + s) % 8
        block = wall.at[m, origin, carried, parity]
        j = slot(way, s)
        return copy(block, block, ring_send.at[m, j], ring_recv.at[m, j],
                    above if way == 0 else below)

    def ring_got(m, way, s):
        block = wall.at[m, place(way, s), carried, parity]
        j = slot(way, s)
        return copy(block, block, ring_send.at[m, j], ring_recv.at[m, j], above)

    def ring_last(m):
        block = wall.at[m, (y + 5 + 6 * c) % 8, carried, parity]
        return copy(block, block, ring_send.at[m, 3], ring_recv.at[m, 3],
                    {"wide": ((y + 1 + 6 * c) % 8) * 4 + zh * 2 + c})

    def cross_copy(m, way, s):
        block = wall.at[m, place(way, s), carried, parity]
        j = slot(way, s)
        to = 1 + 2 * c if s == 3 else (1, 3)[way]
        return copy(block, block, cross_send.at[m, j], cross_recv.at[m, j], at_x(to))

    def cross_got(m, way, s):
        block = wall.at[m, place(way, s), carried, 1 - parity]
        j = slot(way, s)
        return copy(block, block, cross_send.at[m, j], cross_recv.at[m, j], at_x(1))

    def core_copy(m, kind, way, s, mine=True):
        half_of = carried if mine else 1 - carried
        block = wall.at[m, place(way, s), half_of, 1 - parity if kind else parity]
        j = slot(way, s)
        return copy(block, block, core_send.at[m, kind, j], core_recv.at[m, kind, j], partner)

    def core_own(m, core):
        block = wall.at[m, y, zh, core]
        return copy(block, block, core_send.at[m, 0, 7], core_recv.at[m, 0, 7], partner)

    def core_far(m, kind):
        block = wall.at[m, y, 1 - zh, 1 - parity if kind else parity]
        return copy(block, block, core_send.at[m, 1, 7 + kind], core_recv.at[m, 1, 7 + kind],
                    partner)

    def cross_far(m, own=True):
        block = wall.at[m, y, 1 - zh, parity if own else 1 - parity]
        return copy(block, block, cross_send.at[m, 7], cross_recv.at[m, 7], at_x(1))

    def ways_of(s):
        return (0, 1) if s < 3 else (0,)

    def start_stream(m):
        for way in range(2):
            ring_copy(m, way, 0).start()

    def have_own(m):
        core_own(m, 1 - c).wait_recv()

        @pl.when(c == 0)
        def _():
            start_stream(m)

    def begin_far(m):
        start_stream(m)
        core_far(m, 0).start()
        cross_far(m).start()

    def inner_far(m):
        @pl.when((c == 1) & jnp.logical_not(edge))
        def _():
            near_copy(m).wait_recv()

    def have_far(m):
        @pl.when(c == 1)
        def _():
            cross_far(m, False).wait_recv()
            core_far(m, 1).start()

        @pl.when(c == 0)
        def _():
            core_far(m, 0).wait_recv()
            core_far(m, 1).wait_recv()

    def ring_step(m, s):
        for way in ways_of(s):
            ring_got(m, way, s).wait_recv()
            if s < 2:
                ring_copy(m, way, s + 1).start()
            if s == 2:
                @pl.when(c == way)
                def _():
                    ring_last(m).start()
            cross_copy(m, way, s).start()
            core_copy(m, 0, way, s).start()

    def cross_step(m, s):
        for way in ways_of(s):
            cross_got(m, way, s).wait_recv()
            core_copy(m, 1, way, s).start()

    def project(m, origin, first=False):
        term = nn(lhs[origin], wall[m, origin].reshape(192, 768))
        if first:
            acc[m] = term
        else:
            acc[m] += term

    def project_step(m, s):
        for way in ways_of(s):
            for kind in range(2):
                core_copy(m, kind, way, s, False).wait_recv()

            @pl.when(m < OUT)
            def _():
                project(m, place(way, s))

    def spread_copy(m, d):
        return copy(proj.at[m, (zl + d) % 4], recv.at[m, 2 + zl], spread_send.at[m, d - 1],
                    spread_recv.at[m, d - 1], at_z(d))

    def spread_arrived(m, d):
        return copy(proj.at[m, (zl + d) % 4], recv.at[m, 2 + (zl + 4 - d) % 4],
                    spread_send.at[m, d - 1], spread_recv.at[m, d - 1], at_z(d))

    def halo_copy(m, way, arriving=False):
        start = (4, 2)[way]
        into = (0, 6)[way]
        return copy(recv.at[m, start:start + 2], recv.at[m, into:into + 2],
                    halo_send.at[m, way], halo_recv.at[m, way], at_x((1, 3)[way]))

    def ghalo_copy(kv, way):
        return copy(halo_out.at[kv, way], halo_in.at[kv, way], ghalo_send.at[kv, way],
                    ghalo_recv.at[kv, way], at_x((3, 1)[way]))

    def back_copy(t, source, j):
        return copy(source, back.at[t, zl], back_send.at[t, j], back_recv.at[t, zl],
                    {"blk": x * 4 + j})

    def send_back(t, source, j):
        @pl.when(j != zl)
        def _():
            back_copy(t, source, j).start()

        @pl.when(j == zl)
        def _():
            back[t, zl] = source[...]

    def wait_back(t):
        for d in range(1, 4):
            g = (zl + d) % 4
            copy(back.at[t, g], back.at[t, g], back_send.at[t, g], back_recv.at[t, g],
                 {"blk": x * 4 + g}).wait_recv()

    def line_sends(way, k):
        return (zl < 3) & (zl >= k) if way == 0 else (zl > 0) & (zl + k <= 3)

    def line_gets(way, k):
        return zl >= k + 1 if way == 0 else zl + k <= 2

    def line_copy(way, k, part):
        block = up_all.at[zl - k if way == 0 else zl + k, part]
        return copy(block, block, line_send.at[way, k, part], line_recv.at[way, k, part],
                    {"blk": b + 1 if way == 0 else b - 1})

    def line_got(way, k, part):
        block = up_all.at[zl - 1 - k if way == 0 else zl + 1 + k, part]
        return copy(block, block, line_send.at[way, k, part], line_recv.at[way, k, part], partner)

    def line_step(k, part):
        for way in range(2):
            @pl.when(line_gets(way, k))
            def _():
                line_got(way, k, part).wait_recv()

                @pl.when(line_sends(way, k + 1))
                def _():
                    line_copy(way, k + 1, part).start()

    def other_half():
        return copy(up_all.at[:, 1 - c], up_other, swap_send.at[0], swap_recv.at[0], partner)

    def other_mix(j):
        return copy(mix.at[j], mix_other.at[j], swap_send.at[1 + j], swap_recv.at[1 + j], partner)

    def x_copy(d):
        return copy(xs.at[(x + d) % 4], xr.at[d - 1], xs_send.at[d - 1], xs_recv.at[d - 1], at_x(d))

    def y_copy(d):
        return copy(ys.at[(y + d) % 8], yr.at[d - 1], ys_send.at[d - 1], ys_recv.at[d - 1], at_y(d))

    def here_copy():
        return copy(fs.at[zh], fr.at[0], fs_send.at[0], fs_recv.at[0], turned_here)

    def far_piece():
        return copy(fs.at[1 - zh], fr.at[1], fs_send.at[1], fs_recv.at[1], turned_far)

    @pl.when(edge & (c == parity))
    def _():
        for m in range(4):
            far_copy(m).start()

    for m in range(4):
        core_own(m, c).start()
    have_own(0)

    @pl.when(edge & (c == 1))
    def _():
        for m in range(4):
            near_copy(m).wait_recv()
            near_copy(m).start()
            if m == 0:
                begin_far(0)

    load_stream(1).wait()
    by_core = upstream_in[...].T.reshape(16, 2, 48, 128)
    for core in range(2):
        up_all[zl, core] = by_core[:, core].reshape(768, 128).T
    for part in range(2):
        for way in range(2):
            @pl.when(line_sends(way, 0))
            def _():
                line_copy(way, 0, part).start()

    load_stream(0).wait()
    values = second[...].astype(F32)
    center = values - jnp.mean(values, axis=-1, keepdims=True)
    inv_std = lax.rsqrt(jnp.mean(center * center, axis=-1, keepdims=True) + EPSILON)
    unit[...] = center * inv_std
    spread_std[...] = jnp.broadcast_to(inv_std, (128, 128))
    unit_b = unit[...].astype(BF16)
    for i in range(8):
        lhs[i] = unit_b[:, 192 * i:192 * i + 192]

    @pl.when((c == 1) & jnp.logical_not(edge))
    def _():
        near_copy(0).wait_recv()
        begin_far(0)

    def finish(m):
        proj[m] = acc[m].T.astype(BF16).reshape(4, 192, 128)
        for d in range(1, 4):
            spread_copy(m, d).start()
        recv[m, 2 + zl] = proj[m, zl]

    def gather_step(t, _):
        def at(late, f, s, last=OUT):
            m = t - late - s

            @pl.when((m >= 0) & (m <= last))
            def _():
                f(m, s)

        for s in (3, 2, 1, 0):
            at(0, ring_step, s)
        for s in (3, 2, 1, 0):
            at(1, cross_step, s)

        @pl.when(t < 3)
        def _():
            have_own(t + 1)
            inner_far(t + 1)

            @pl.when(c == 1)
            def _():
                begin_far(t + 1)

        @pl.when(t < 6)
        def _():
            line_step(t // 2, t % 2)

        at(1, lambda m, s: have_far(m), 0)
        at(1, lambda m, s: project(m, y, True), 0, QUERY)
        for s in (3, 2, 1, 0):
            at(1, project_step, s)
        at(4, lambda m, s: finish(m), 0, QUERY)

        @pl.when(t == 6)
        def _():
            other_half().start()

        @pl.when(t >= 6)
        def _():
            m = t - 6
            for d in range(1, 4):
                spread_arrived(m, d).wait_recv()
            for way in range(2):
                halo_copy(m, way).start()

        return 0

    lax.fori_loop(0, 8, gather_step, 0)

    columns = pl.ds(pl.multiple_of((zl // 2) * 384, 128), 384)
    dm_all[...] = sum(
        nn(up_all[:, core].reshape(512, 768), wall[OUT, :, :, core, :, columns].reshape(768, 384))
        for core in range(2)).T.astype(BF16)
    dm[...] = dm_all[pl.ds(pl.multiple_of((zl % 2) * 192, 64), 192), :]

    for m in (KEY, VALUE):
        for way in range(2):
            halo_copy(m, way).wait_recv()
    for e in range(8):
        for m, natural, turned in ((KEY, kn, kt), (VALUE, vn, vt)):
            block = recv[m, e]
            flat = block.T
            for h in range(3):
                turned[h, :, 128 * e:128 * e + 128] = block[64 * h:64 * h + 64]
                natural[h, 128 * e:128 * e + 128, :] = flat[:, 64 * h:64 * h + 64]

    scale = HDIM ** -0.5
    dkv[...] = jnp.zeros_like(dkv)

    def window(j):
        return pl.ds(pl.multiple_of(j * 128, 128), 640)

    def of_block(j):
        return pl.ds(pl.multiple_of(j * 128, 128), 128)

    def forward(i, _):
        j = (zl + 4 - i) % 4

        @pl.when(i > 0)
        def _():
            spread_arrived(QUERY, i).wait_recv()

        for h in range(3):
            rows = slice(64 * h, 64 * h + 64)
            scores = nn(kn[h, window(j), :], recv[QUERY, 2 + j, rows, :] * scale)
            exps = jnp.exp(scores - jnp.max(scores, axis=0, keepdims=True))
            weights = (exps * (1 / jnp.sum(exps, axis=0, keepdims=True))).astype(BF16)
            probs[j, h] = weights
            mix[j, rows, :] = nn(vt[h, :, window(j)], weights).astype(BF16)
            dkv[1, h, :, window(j)] += nt(dm[rows, of_block(j)], weights)
        other_mix(j).start()
        send_back(MIX, mix.at[j], j)
        return 0

    def backward(j, _):
        for h in range(3):
            rows = slice(64 * h, 64 * h + 64)
            dmh = dm[rows, of_block(j)] * scale
            delta = jnp.sum(dmh.astype(F32) * mix[j, rows, :].astype(F32), axis=0, keepdims=True)
            d_weights = nn(vn[h, window(j), :], dmh)
            d_scores = (probs[j, h].astype(F32) * (d_weights - delta)).astype(BF16)
            dq[j, rows, :] = nn(kt[h, :, window(j)], d_scores).astype(BF16)
            dkv[0, h, :, window(j)] += nt(recv[QUERY, 2 + j, rows, :], d_scores)
        send_back(DQ, dq.at[j], j)
        return 0

    def send_halo(kv, way):
        lanes = slice(0, 256) if way == 0 else slice(768, 1024)
        halo_out[kv, way] = dkv[kv, :, :, lanes].astype(BF16).reshape(192, 256)
        ghalo_copy(kv, way).start()

    def finish_halo(kv):
        for way in range(2):
            ghalo_copy(kv, way).wait_recv()
            for i in range(2):
                j = i + 2 - 2 * way
                got = halo_in[kv, way, :, 128 * i:128 * i + 128].astype(F32)
                own = dkv[kv, :, :, 256 + 128 * j:384 + 128 * j].reshape(192, 128)
                dkv_out[kv, j] = (own + got).astype(BF16)
                send_back(DK + kv, dkv_out.at[kv, j], j)

    lax.fori_loop(0, 4, forward, 0)
    for way in range(2):
        send_halo(1, way)
    lax.fori_loop(0, 2, backward, 0)
    send_halo(0, 0)

    other_half().wait_recv()
    for j in range(4):
        other_mix(j).wait_recv()
    rows = sum(
        nn(jnp.concatenate([mix[j], mix_other[j]], axis=1),
           jnp.concatenate([up_all[j, c], up_other[j]], axis=0)) for j in range(4))
    xs[...] = rows.astype(BF16).reshape(4, 48, 768)
    for d in range(1, 4):
        x_copy(d).start()

    lax.fori_loop(2, 4, backward, 0)
    send_halo(0, 1)
    finish_halo(1)

    def drain(m, _):
        @pl.when(edge & (c == parity))
        def _():
            far_copy(m).wait_send()

        @pl.when(edge & (c == 1))
        def _():
            near_copy(m).wait_send()

        @pl.when(c == 1)
        def _():
            cross_far(m).wait_send()
            for kind in range(2):
                core_far(m, kind).wait_send()

        core_own(m, c).wait_send()
        for s in range(4):
            for way in ways_of(s):
                if s < 3:
                    ring_copy(m, way, s).wait_send()
                else:
                    ring_last(m).wait_send()
                cross_copy(m, way, s).wait_send()
                for kind in range(2):
                    core_copy(m, kind, way, s).wait_send()
        for d in range(1, 4):
            @pl.when(m < OUT)
            def _():
                spread_copy(m, d).wait_send()

        return 0

    def natural(t):
        return back[t].reshape(768, 128).T

    lax.fori_loop(0, 4, drain, 0)

    for d in range(1, 4):
        x_copy(d).wait_recv()
    part = xs[x].astype(F32)
    for d in range(3):
        part = part + xr[d].astype(F32)
    for i in range(8):
        ys[i] = part[:, 96 * i:96 * i + 96].astype(BF16)
    for d in range(1, 8):
        y_copy(d).start()

    finish_halo(0)

    wait_back(MIX)
    load_stream(2).wait()
    mixture = natural(MIX)
    for i in range(4):
        lanes = slice(384 * i, 384 * i + 384)
        branch = nt(mixture, wall[OUT, 2 * i:2 * i + 2].reshape(384, 768))
        x_ref[0, :, lanes] = (first[:, lanes].astype(F32) - branch).astype(BF16)

    def add_unit(t, m, first=False):
        wait_back(t)
        grads = natural(t)
        for i in range(4):
            lanes = slice(384 * i, 384 * i + 384)
            term = nt(grads, wall[m, 2 * i:2 * i + 2].reshape(384, 768))
            if first:
                d_unit[:, lanes] = term
            else:
                d_unit[:, lanes] += term

    add_unit(DQ, QUERY, True)
    add_unit(DV, VALUE)

    for d in range(1, 8):
        y_copy(d).wait_recv()
    part = ys[y].astype(F32)
    for d in range(7):
        part = part + yr[d].astype(F32)
    for i in range(2):
        fs[i] = part[:, 48 * i:48 * i + 48]
    far_piece().start()

    @pl.when(x != zl)
    def _():
        here_copy().start()

    @pl.when(x == zl)
    def _():
        fr[0] = fs[zh]

    add_unit(DK, KEY)
    grads = d_unit[...]
    kept = unit[...]
    correction = (grads - jnp.mean(grads, axis=-1, keepdims=True)
                  - kept * jnp.mean(grads * kept, axis=-1, keepdims=True))
    load_stream(3).wait()
    dx_ref[0] = (dsecond[...].astype(F32) + spread_std[:, :1] * correction).astype(BF16)

    far_piece().wait_recv()

    @pl.when(x != zl)
    def _():
        here_copy().wait_recv()

    grad_ref[...] = (fr[0] + fr[1]) / 32

    for kv in range(2):
        for way in range(2):
            halo_copy(kv, way).wait_send()
            ghalo_copy(kv, way).wait_send()
    other_half().wait_send()
    for j in range(4):
        other_mix(j).wait_send()
    for t in (MIX, DQ, DK, DV):
        for d in range(1, 4):
            g = (zl + d) % 4
            back_copy(t, mix.at[g], g).wait_send()
    for d in range(1, 4):
        x_copy(d).wait_send()
    for d in range(1, 8):
        y_copy(d).wait_send()
    far_piece().wait_send()

    @pl.when(x != zl)
    def _():
        here_copy().wait_send()

    for way in range(2):
        for k in range(3):
            @pl.when(line_sends(way, k))
            def _():
                for part in range(2):
                    line_copy(way, k, part).wait_send()


def block(y_first, y_second, upstream, dy_second, in_proj, out_t):
    vmem = pl.BlockSpec(memory_space=pltpu.VMEM)
    dma = pltpu.SemaphoreType.DMA
    stream = jax.ShapeDtypeStruct((1, 128, 1536), BF16)
    return pl.pallas_call(
        kernel,
        out_shape=(stream, stream, jax.ShapeDtypeStruct((48, 48), F32)),
        in_specs=[pl.BlockSpec(memory_space=pl.ANY)] * 6,
        out_specs=(vmem,) * 3,
        scratch_shapes=[
            pltpu.VMEM((128, 1536), BF16),
            pltpu.VMEM((128, 1536), BF16),
            pltpu.VMEM((128, 1536), BF16),
            pltpu.VMEM((128, 1536), BF16),
            pltpu.VMEM((128, 1536), F32),
            pltpu.VMEM((128, 128), F32),
            pltpu.VMEM((4, 8, 2, 2, 48, 768), BF16),
            pltpu.VMEM((8, 128, 192), BF16),
            pltpu.VMEM((3, 128, 768), F32),
            pltpu.VMEM((3, 4, 192, 128), BF16),
            pltpu.VMEM((3, 8, 192, 128), BF16),
            pltpu.VMEM((3, 1024, 64), BF16),
            pltpu.VMEM((3, 1024, 64), BF16),
            pltpu.VMEM((3, 64, 1024), BF16),
            pltpu.VMEM((3, 64, 1024), BF16),
            pltpu.VMEM((4, 3, 640, 128), BF16),
            pltpu.VMEM((4, 192, 128), BF16),
            pltpu.VMEM((4, 192, 128), BF16),
            pltpu.VMEM((2, 3, 64, 1024), F32),
            pltpu.VMEM((2, 2, 192, 256), BF16),
            pltpu.VMEM((2, 2, 192, 256), BF16),
            pltpu.VMEM((2, 4, 192, 128), BF16),
            pltpu.VMEM((4, 4, 192, 128), BF16),
            pltpu.VMEM((128, 1536), F32),
            pltpu.VMEM((4, 2, 128, 768), BF16),
            pltpu.VMEM((4, 128, 768), BF16),
            pltpu.VMEM((4, 192, 128), BF16),
            pltpu.VMEM((384, 512), BF16),
            pltpu.VMEM((192, 512), BF16),
            pltpu.VMEM((4, 48, 768), BF16),
            pltpu.VMEM((3, 48, 768), BF16),
            pltpu.VMEM((8, 48, 96), BF16),
            pltpu.VMEM((7, 48, 96), BF16),
            pltpu.VMEM((2, 48, 48), F32),
            pltpu.VMEM((2, 48, 48), F32),
            dma((4,)), dma((4,)),
            dma((4,)), dma((4,)), dma((4,)),
            dma((4, 7)), dma((4, 7)),
            dma((4, 8)), dma((4, 8)),
            dma((4, 2, 9)), dma((4, 2, 9)),
            dma((2, 3, 2)), dma((2, 3, 2)),
            dma((5,)), dma((5,)),
            dma((3, 3)), dma((3, 3)),
            dma((2, 2)), dma((2, 2)),
            dma((2, 2)), dma((2, 2)),
            dma((4, 4)), dma((4, 4)),
            dma((3,)), dma((3,)),
            dma((7,)), dma((7,)),
            dma((2,)), dma((2,)),
        ],
        compiler_params=pltpu.CompilerParams(
            collective_id=0, has_side_effects=True, vmem_limit_bytes=62 * 2**20),
        name="attention_block_backward",
    )(y_first, y_second, upstream, dy_second, in_proj, out_t)


def hand_over(x_ref, dx_ref, grad_ref, x_out, dx_out, grad_out):
    x_out[...] = x_ref[...]
    dx_out[...] = dx_ref[...]
    grad_out[...] = grad_ref[...]


def body(y_first, y_second, first_output_cotangent, dy_second, in_proj, out_proj):
    made = block(y_first, y_second, first_output_cotangent, dy_second, in_proj, out_proj.T)
    vmem = pl.BlockSpec(memory_space=pltpu.VMEM)
    return pl.pallas_call(
        hand_over,
        out_shape=tuple(jax.ShapeDtypeStruct(a.shape, a.dtype) for a in made),
        in_specs=[vmem] * 3,
        out_specs=(vmem,) * 3,
        name="hand_over",
    )(*made)


def solution(mesh):
    placed = (
        P("wide", "blk", None),
        P("wide", "blk", None),
        P("wide", "blk", None),
        P("wide", "blk", None),
        P(None, "wide", None),
        P(None, "wide"),
    )
    return jax.shard_map(
        body,
        mesh=mesh,
        in_specs=placed,
        out_specs=(P("wide", "blk", None), P("wide", "blk", None), P("blk", "wide")),
        check_vma=False,
    )
```
